512 devices in a mesh: dp: 64 (over y, x, core), mp: 8 (over z).
Axes of the slice: x: 4, y: 8, z: 8, core: 2. Of those that a mesh axis runs over, the one named last changes fastest.
Arguments:
- up_grad: bfloat16 [64, 64, 28672], P('dp', None, 'mp'), may hold values from -60 to 60, as said below
- up_error: float32 [64, 64, 28672], P('dp', None, 'mp'), may hold values from -4 to 4
- up_warm: float32 [28672, 32], P('mp'), may hold values from -0.03125 to 0.03125
- down_grad: bfloat16 [64, 128, 8192], P('dp', None, 'mp'), may hold values from -60 to 60, as said below
- down_error: float32 [64, 128, 8192], P('dp', None, 'mp'), may hold values from -4 to 4
- down_warm: float32 [8192, 32], P('mp'), may hold values from -0.0625 to 0.0625
Outputs:
- up_average: bfloat16 [64, 28672], P(None, 'mp')
- up_residue: float32 [64, 64, 28672], P('dp', None, 'mp')
- down_average: bfloat16 [128, 8192], P(None, 'mp')
- down_residue: float32 [64, 128, 8192], P('dp', None, 'mp')
The draws below stay inside these ranges and needn't reach their ends.
Inputs may be any that keep to these rules, and one draw needn't show every extreme that they name: `up_grad`: each replica's up gradient rows. `down_grad`: each replica's down gradient rows.
All inputs are finite; a program needn't handle non-finite values.
Results may differ from the reference program's by a relative error of at most 0.0011.
Values sent between devices are 32-bit elements; how exact they have to be, the bound alone decides.
A program may use at most 64 MiB of HBM per device.

```python
import jax
import jax.numpy as jnp
from jax import lax

DM = 8192
FF = 28672
RANK = 32
RU = 64
RD = 128
N_DP = 64


def replica_field(key, reps, rows, row_top):
    keys = jax.random.split(key, 2)
    ramp = jnp.exp(jnp.log(3.0) * jnp.arange(reps, dtype=jnp.float32) / max(reps - 1, 1))
    row_scale = jnp.exp(jax.random.uniform(keys[1], (1, rows, 1), jnp.float32) * jnp.log(row_top))
    return (keys[0], ramp[:, None, None] * row_scale / 3.0)


def draw_up_grad(key, part):
    key = jax.random.fold_in(key, 11)
    inner, scale = replica_field(key, N_DP, RU, 10.0)
    base = jnp.clip(jax.random.normal(inner, (N_DP, RU, FF), jnp.float32), -6.0, 6.0)
    return jnp.clip(base * scale, -60.0, 60.0).astype(jnp.bfloat16)


def draw_down_grad(key, part):
    key = jax.random.fold_in(key, 23)
    inner, scale = replica_field(key, N_DP, RD, 10.0)
    base = jnp.clip(jax.random.normal(inner, (N_DP, RD, DM), jnp.float32), -6.0, 6.0)
    return jnp.clip(base * scale, -60.0, 60.0).astype(jnp.bfloat16)


def steps_of(key, extent, cuts, low, top_value):
    def one(position, shards_of):
        steps = jax.random.uniform(jax.random.fold_in(jax.random.fold_in(key, 6), position), (shards_of,), jnp.float32, low / len(cuts), top_value / len(cuts))
        return jnp.repeat(jnp.exp(steps), extent[position] // shards_of).reshape((-1,) + (1,) * (len(extent) - position - 1))

    loudness = one(*cuts[0])
    for cut in cuts[1:]:
        loudness = loudness * one(*cut)
    return loudness


def bell_draw(stream_key, extent, spread, bound, cuts=(), kind=jnp.bfloat16):
    entries = spread * jax.random.normal(stream_key, extent, jnp.float32)
    if cuts:
        entries = entries * steps_of(stream_key, extent, cuts, -0.22, 0.18)
    return jnp.clip(entries, -bound, bound).astype(kind)


def setup_inputs(seed: int = 0) -> dict:
    streams_of = jax.random.split(jax.random.key(seed), 7)
    up_grad = draw_up_grad(jax.random.fold_in(streams_of[6], 71), 0)
    up_error = bell_draw(streams_of[1], (N_DP, RU, FF), 0.5, 4.0, ((0, 64), (2, 8)), jnp.float32)
    up_warm = bell_draw(streams_of[2], (FF, RANK), FF ** -0.5, 0.03125, ((0, 8),), jnp.float32)
    down_grad = draw_down_grad(jax.random.fold_in(streams_of[6], 71), 0)
    down_error = bell_draw(streams_of[4], (N_DP, RD, DM), 0.5, 4.0, ((0, 64), (2, 8)), jnp.float32)
    down_warm = bell_draw(streams_of[5], (DM, RANK), DM ** -0.5, 0.0625, ((0, 8),), jnp.float32)
    return dict(up_grad=up_grad, up_error=up_error, up_warm=up_warm, down_grad=down_grad, down_error=down_error, down_warm=down_warm)


def compress(grads, errors, warm):
    hi = lax.Precision.HIGHEST
    merged = grads.astype(jnp.float32) + errors
    proj = jnp.einsum('nrc,ck->rk', merged, warm, precision=hi)
    gram = jnp.dot(proj.T, proj, precision=hi)
    chol = jnp.linalg.cholesky(gram)
    ortho = lax.linalg.triangular_solve(chol, proj, left_side=False, lower=True, transpose_a=True)
    back = jnp.einsum('nrc,rk->ck', merged, ortho, precision=hi) / N_DP
    delta = jnp.dot(ortho, back.T, precision=hi)
    return (delta.astype(jnp.bfloat16), merged - delta[None])

def reference(up_grad, up_error, up_warm, down_grad, down_error, down_warm):
    up_average, up_residue = compress(up_grad, up_error, up_warm)
    down_average, down_residue = compress(down_grad, down_error, down_warm)
    return (up_average, up_residue, down_average, down_residue)
```

```python
import jax
import jax.numpy as jnp
from jax import lax
from jax.experimental import pallas as pl
from jax.experimental.pallas import tpu as pltpu
from jax.sharding import PartitionSpec as P

F32 = jnp.float32
BF16 = jnp.bfloat16
HI = lax.Precision.HIGHEST
MESH = pl.DeviceIdType.MESH
NY, NX, NC, NZ = 8, 4, 2, 8
RANK = 32
UP_R, UP_C = 64, 3584
DN_R, DN_C = 128, 1024
HALF = UP_C // 2
SH = 48
FR = 24


def nt(a, b, precision=None):
    return lax.dot_general(a, b, (((1,), (1,)), ((), ())), preferred_element_type=F32, precision=precision)


def split(a):
    hi = a.astype(BF16)
    return hi, (a - hi.astype(F32)).astype(BF16)


def nt3(a, b):
    ah, al = split(a)
    bh, bl = split(b)
    return nt(ah, bh) + nt(ah, bl) + nt(al, bh)


def eliminate(a1, a2):
    shape = (RANK, 128)
    row = lax.broadcasted_iota(jnp.int32, shape, 0)
    lane = lax.broadcasted_iota(jnp.int32, shape, 1)
    in_dn = lane >= 96
    scale_u = jnp.ones(shape, F32)
    scale_d = jnp.ones(shape, F32)
    for panel in range(4):
        first = panel * 8
        cu = [jnp.broadcast_to(a1[:, 64 + first + m:65 + first + m], shape) for m in range(8)]
        cd = [jnp.broadcast_to(a1[:, 96 + first + m:97 + first + m], shape) for m in range(8)]
        for m in range(8):
            k = first + m
            below = row > k
            pu = cu[m][k:k + 1, :]
            pd = cd[m][k:k + 1, :]
            fu = jnp.where(below, cu[m] * (1.0 / pu), 0.0)
            fd = jnp.where(below, cd[m] * (1.0 / pd), 0.0)
            for n in range(m + 1, 8):
                cu[n] = cu[n] - fu * cu[n][k:k + 1, :]
                cd[n] = cd[n] - fd * cd[n][k:k + 1, :]
            a1 = a1 - jnp.where(in_dn, fd, fu) * a1[k:k + 1, :]
            a2 = a2 - fd * a2[k:k + 1, :]
            scale_u = jnp.where(row == k, lax.rsqrt(pu), scale_u)
            scale_d = jnp.where(row == k, lax.rsqrt(pd), scale_d)
    return a1 * scale_u, a2 * scale_d


def exchange(ug, ue, uw, dg, de, dw, f_out, wu_out, wd_out,
             vug, vue, vuw, vdg, vde, vdw, T, Rc, Rx, Ry, FG,
             pt, pc, px, pxr, pz, py, pg,
             in_sem, s_mc, r_mc, s_mx, r_mx, s_my, r_my,
             s_pc, r_pc, s_px, r_px, s_pz, r_pz, s_py, r_py, s_pa, r_pa, s_pb, r_pb,
             s_fy, r_fy, s_fx, r_fx, s_fc, r_fc, out_sem):
    d = lax.axis_index("dp")
    z = lax.axis_index("mp")
    c = lax.rem(d, 2)
    x = lax.rem(lax.div(d, 2), NX)
    y = lax.div(d, 8)

    def at(yy, xx, cc):
        return ((yy * NX + xx) * NC + cc, z)

    partner = at(y, x, 1 - c)

    def xpeer(o):
        return at(y, lax.rem(x + o, NX), c)

    def ypeer(o):
        return at(lax.rem(y + o, NY), x, c)

    def zpeer(o):
        return (d, lax.rem(z + o, NZ))

    bar = pltpu.get_barrier_semaphore()
    pl.semaphore_signal(bar, 1, device_id=partner, device_id_type=MESH)
    for o in range(1, NZ):
        pl.semaphore_signal(bar, 1, device_id=zpeer(o), device_id_type=MESH)
    for o in range(1, NY):
        pl.semaphore_signal(bar, 1, device_id=ypeer(o), device_id_type=MESH)
    for o in range(1, NX):
        pl.semaphore_signal(bar, 1, device_id=xpeer(o), device_id_type=MESH)

    loads = [pltpu.make_async_copy(a, b, in_sem.at[i])
             for i, (a, b) in enumerate([(ug, vug), (ue, vue), (uw, vuw), (dg, vdg), (de, vde), (dw, vdw)])]
    for cp in loads:
        cp.start()

    for cp in loads[:3]:
        cp.wait()
    acc = jnp.zeros((RANK, UP_R), F32)
    for b in range(HALF // 256):
        parts = []
        for half in range(2):
            cols = pl.ds(half * HALF + 256 * b, 256)
            m = vug[:, cols].astype(F32) + vue[:, cols]
            acc += nt3(vuw[:, cols], m)
            parts.append(m)
        stacked = jnp.concatenate(parts, axis=0)
        for s in range(2):
            turned = stacked[:, 128 * s:128 * (s + 1)].T
            for i in range(16):
                tile = (2 * b + s) * 16 + i
                q, u = tile // 7, tile % 7
                rows = turned[8 * i:8 * i + 8, :]
                if u <= 3:
                    T[0, q // NY, q % NY, 8 * u:8 * u + 8, :] = rows
                if u >= 3:
                    T[1, q // NY, q % NY, 8 * (u - 3):8 * (u - 3) + 8, :] = rows
    pt[0:32, :] = jnp.concatenate([acc, jnp.zeros((RANK, 64), F32)], axis=1)
    for cp in loads[3:]:
        cp.wait()
    acc = jnp.zeros((RANK, DN_R), F32)
    for b in range(DN_C // 256):
        cols = pl.ds(256 * b, 256)
        m = vdg[:, cols].astype(F32) + vde[:, cols]
        acc += nt3(vdw[:, cols], m)
        for s in range(2):
            turned = m[:, 128 * s:128 * (s + 1)].T
            for i in range(16):
                tile = (2 * b + s) * 16 + i
                q, u = tile // 4, tile % 4
                T[u // 2, q // NY, q % NY, 32 + 8 * (u % 2):40 + 8 * (u % 2), :] = turned[8 * i:8 * i + 8, :]
    pt[32:64, :] = acc

    pl.semaphore_wait(bar, 1 + 7 + 7 + 3)

    def remote(src, dst, ssem, rsem, dev):
        cp = pltpu.make_async_remote_copy(src_ref=src, dst_ref=dst, send_sem=ssem, recv_sem=rsem,
                                          device_id=dev, device_id_type=MESH)
        cp.start()
        return cp

    sent = []
    cp_pc = remote(pt.at[pl.ds((1 - c) * 32, 32)], pc, s_pc, r_pc, partner)
    sent.append(cp_pc)
    order = [1, 3, 2, 0]
    cp_mc = {}
    for o in order:
        xx = lax.rem(x + o, NX)
        cp_mc[o] = remote(T.at[1 - c, xx], Rc.at[xx], s_mc.at[o], r_mc.at[o], partner)
        sent.append(cp_mc[o])
    cp_pc.wait_recv()
    px[...] = pt[pl.ds(pl.multiple_of(c * 32, 32), 32), :] + pc[...]
    cp_px = [remote(px.at[pl.ds(lax.rem(x + o, NX) * 8, 8)], pxr.at[o - 1], s_px.at[o - 1], r_px.at[o - 1], xpeer(o))
             for o in (1, 2, 3)]
    sent += cp_px
    cp_mx = []
    for o in order:
        xx = lax.rem(x + o, NX)
        cp_mc[o].wait_recv()
        T[c, xx] = T[c, xx] + Rc[xx]
        if o:
            cp_mx.append(remote(T.at[c, xx], Rx.at[o - 1], s_mx.at[o - 1], r_mx.at[o - 1], xpeer(o)))
    sent += cp_mx
    for cp in cp_px:
        cp.wait_recv()
    pz[z] = (px[pl.ds(pl.multiple_of(x * 8, 8), 8), :] + pxr[0]) + (pxr[1] + pxr[2])
    cp_pz = [remote(pz.at[z], pz.at[z], s_pz.at[o - 1], r_pz.at[o - 1], zpeer(o)) for o in range(1, NZ)]
    sent += cp_pz
    for cp in cp_pz:
        cp.wait_recv()
    py[y] = ((pz[0] + pz[1]) + (pz[2] + pz[3])) + ((pz[4] + pz[5]) + (pz[6] + pz[7]))
    cp_py = [remote(py.at[y], py.at[y], s_py.at[o - 1], r_py.at[o - 1], ypeer(o)) for o in range(1, NY)]
    sent += cp_py
    for cp in cp_py:
        cp.wait_recv()
    mine = pl.ds(pl.multiple_of(x * 8, 8), 8)
    pg[c, mine, :] = ((py[0] + py[1]) + (py[2] + py[3])) + ((py[4] + py[5]) + (py[6] + py[7]))
    cp_pa = [remote(pg.at[c, mine], pg.at[c, mine], s_pa.at[o - 1], r_pa.at[o - 1], xpeer(o)) for o in (1, 2, 3)]
    sent += cp_pa

    for cp in cp_mx:
        cp.wait_recv()
    cp_my = []
    for o in (4, 3, 5, 2, 6, 1, 7, 0):
        yy = lax.rem(y + o, NY)
        T[c, x, yy] = (T[c, x, yy] + Rx[0, yy]) + (Rx[1, yy] + Rx[2, yy])
        if o:
            cp_my.append(remote(T.at[c, x, yy], Ry.at[o - 1], s_my.at[o - 1], r_my.at[o - 1], ypeer(o)))
    sent += cp_my

    for cp in cp_pa:
        cp.wait_recv()
    cp_pb = remote(pg.at[c], pg.at[c], s_pb, r_pb, partner)
    sent.append(cp_pb)
    cp_pb.wait_recv()

    a1 = pg[0]
    a2 = pg[1]
    gu = nt(a1, a1, HI)
    gd = nt(a2, a2, HI)
    a1, a2 = eliminate(jnp.concatenate([a1[:, :64], gu, gd], axis=1), a2)
    lane = lax.broadcasted_iota(jnp.int32, (RANK, 128), 1)
    left = jnp.where(lane < 64, a1, 0.0)
    right = pltpu.roll(left, 64, axis=1)
    wu = jnp.concatenate([left, right, left, right], axis=0)
    wd = jnp.concatenate([a2, a2, a2, a2], axis=0)
    wu_out[...] = wu.T
    wd_out[...] = wd.T

    for cp in cp_my:
        cp.wait_recv()
    shard = T[c, x, y]
    for o in range(1, NY):
        shard = shard + Ry[o - 1]
    shard = shard * (1.0 / 64.0)
    ru = nt(shard[0:32], wu, HI)
    rd = nt(shard[32:48], wd, HI)
    lane16 = lax.broadcasted_iota(jnp.int32, (16, 128), 1)
    FG[c, x, y, 0:16, :] = jnp.where(lane16 < 64, ru[0:16], ru[16:32])
    FG[c, x, y, 16:24, :] = jnp.where(lane16[0:8] < 32, rd[0:8], rd[8:16])

    cp_fy = [remote(FG.at[c, x, y], FG.at[c, x, y], s_fy.at[o - 1], r_fy.at[o - 1], ypeer(o)) for o in (4, 3, 5, 2, 6, 1, 7)]
    sent += cp_fy
    for cp in cp_fy:
        cp.wait_recv()
    cp_fx = [remote(FG.at[c, x], FG.at[c, x], s_fx.at[o - 1], r_fx.at[o - 1], xpeer(o)) for o in (2, 1, 3)]
    sent += cp_fx
    cp_fc = [remote(FG.at[c, x], FG.at[c, x], s_fc.at[0], r_fc.at[0], partner)]
    for cp, o in zip(cp_fx, (2, 1, 3)):
        cp.wait_recv()
        xx = lax.rem(x - o + NX, NX)
        cp_fc.append(remote(FG.at[c, xx], FG.at[c, xx], s_fc.at[o], r_fc.at[o], partner))
    sent += cp_fc
    for cp in cp_fc:
        cp.wait_recv()
    cp_out = pltpu.make_async_copy(FG, f_out, out_sem)
    cp_out.start()
    for cp in sent:
        cp.wait_send()
    cp_out.wait()


def finish(f, wu, wd, ug, ue, dg, de, ua, ur, da, dr, fu, fd):
    lane = lax.broadcasted_iota(jnp.int32, (8, 128), 1)
    for tile in range(HALF // 8):
        q, u = tile // 7, tile % 7
        core, s = (0, u) if u <= 3 else (1, u - 3)
        r0 = (s % 2) * 8
        rows = f[core, q // NY, q % NY, r0:r0 + 8, :]
        fu[8 * tile:8 * tile + 8, :] = jnp.where(lane // 64 == s // 2, rows, 0.0)
    for tile in range(DN_C // 8):
        q, u = tile // 4, tile % 4
        rows = f[u // 2, q // NY, q % NY, 16:24, :]
        fd[8 * tile:8 * tile + 8, :] = jnp.where(lane // 32 == u % 2, rows, 0.0)
    for b in range(HALF // 256):
        delta = nt3(wu[...], fu[256 * b:256 * b + 256, :])
        for half in range(2):
            cols = pl.ds(half * HALF + 256 * b, 256)
            part = delta[64 * half:64 * half + 64, :]
            ua[:, cols] = part.astype(BF16)
            ur[:, cols] = (ug[:, cols].astype(F32) + ue[:, cols]) - part
    for b in range(DN_C // 256):
        cols = pl.ds(256 * b, 256)
        delta = nt3(wd[...], fd[256 * b:256 * b + 256, :])
        da[:, cols] = delta.astype(BF16)
        dr[:, cols] = (dg[:, cols].astype(F32) + de[:, cols]) - delta


def body(up_grad, up_error, up_warm, down_grad, down_error, down_warm):
    ug, ue, dg, de = up_grad[0], up_error[0], down_grad[0], down_error[0]
    vm = pl.BlockSpec(memory_space=pltpu.VMEM)
    hbm = pl.BlockSpec(memory_space=pl.ANY)
    dma = pltpu.SemaphoreType.DMA
    V = pltpu.VMEM
    f, wu, wd = pl.pallas_call(
        exchange,
        out_shape=(
            jax.ShapeDtypeStruct((NC, NX, NY, FR, 128), F32),
            jax.ShapeDtypeStruct((128, 128), F32),
            jax.ShapeDtypeStruct((128, 128), F32),
        ),
        in_specs=[hbm] * 6,
        out_specs=(hbm, vm, vm),
        scratch_shapes=[
            V((UP_R, UP_C), BF16), V((UP_R, UP_C), F32), V((RANK, UP_C), F32),
            V((DN_R, DN_C), BF16), V((DN_R, DN_C), F32), V((RANK, DN_C), F32),
            V((NC, NX, NY, SH, 128), F32), V((NX, NY, SH, 128), F32), V((NX - 1, NY, SH, 128), F32),
            V((NY - 1, SH, 128), F32), V((NC, NX, NY, FR, 128), F32),
            V((64, 128), F32), V((32, 128), F32), V((32, 128), F32), V((3, 8, 128), F32),
            V((NZ, 8, 128), F32), V((NY, 8, 128), F32), V((2, 32, 128), F32),
            dma((6,)), dma((4,)), dma((4,)), dma((3,)), dma((3,)), dma((7,)), dma((7,)),
            dma, dma, dma((3,)), dma((3,)), dma((7,)), dma((7,)), dma((7,)), dma((7,)), dma((3,)), dma((3,)), dma, dma,
            dma((7,)), dma((7,)), dma((3,)), dma((3,)), dma((4,)), dma((4,)), dma,
        ],
        compiler_params=pltpu.CompilerParams(
            collective_id=0, has_side_effects=True, vmem_limit_bytes=32 * 1024 * 1024),
        name="exchange",
    )(ug, ue, up_warm.T, dg, de, down_warm.T)
    ua, ur, da, dr = pl.pallas_call(
        finish,
        out_shape=(
            jax.ShapeDtypeStruct((UP_R, UP_C), BF16),
            jax.ShapeDtypeStruct((UP_R, UP_C), F32),
            jax.ShapeDtypeStruct((DN_R, DN_C), BF16),
            jax.ShapeDtypeStruct((DN_R, DN_C), F32),
        ),
        in_specs=[vm] * 7,
        out_specs=(vm,) * 4,
        scratch_shapes=[V((HALF, 128), F32), V((DN_C, 128), F32)],
        compiler_params=pltpu.CompilerParams(vmem_limit_bytes=32 * 1024 * 1024),
        name="finish",
    )(f, wu, wd, ug, ue, dg, de)
    return ua, ur[None], da, dr[None]


def solution(mesh):
    return jax.shard_map(
        body,
        mesh=mesh,
        in_specs=(
            P("dp", None, "mp"),
            P("dp", None, "mp"),
            P("mp", None),
            P("dp", None, "mp"),
            P("dp", None, "mp"),
            P("mp", None),
        ),
        out_specs=(P(None, "mp"), P("dp", None, "mp"), P(None, "mp"), P("dp", None, "mp")),
        check_vma=False,
    )
```

```python
import jax
import jax.numpy as jnp
from jax import lax
from jax.experimental import pallas as pl
from jax.experimental.pallas import tpu as pltpu
from jax.sharding import PartitionSpec as P

F32 = jnp.float32
BF16 = jnp.bfloat16
HI = lax.Precision.HIGHEST
MESH = pl.DeviceIdType.MESH
NY, NX, NC, NZ = 8, 4, 2, 8
RANK = 32
UP_R, UP_C = 64, 3584
DN_R, DN_C = 128, 1024
HALF = UP_C // 2


def nt(a, b, precision=None):
    return lax.dot_general(a, b, (((1,), (1,)), ((), ())), preferred_element_type=F32, precision=precision)


def split(a):
    hi = a.astype(BF16)
    return hi, (a - hi.astype(F32)).astype(BF16)


def nt3(a, b):
    ah, al = split(a)
    bh, bl = split(b)
    return nt(ah, bh) + nt(ah, bl) + nt(al, bh)


def eliminate(a1, a2):
    shape = (RANK, 128)
    row = lax.broadcasted_iota(jnp.int32, shape, 0)
    lane = lax.broadcasted_iota(jnp.int32, shape, 1)
    in_dn = lane >= 96
    scale_u = jnp.ones(shape, F32)
    scale_d = jnp.ones(shape, F32)
    for panel in range(4):
        first = panel * 8
        cu = [jnp.broadcast_to(a1[:, 64 + first + m:65 + first + m], shape) for m in range(8)]
        cd = [jnp.broadcast_to(a1[:, 96 + first + m:97 + first + m], shape) for m in range(8)]
        for m in range(8):
            k = first + m
            below = row > k
            pu = cu[m][k:k + 1, :]
            pd = cd[m][k:k + 1, :]
            fu = jnp.where(below, cu[m] * (1.0 / pu), 0.0)
            fd = jnp.where(below, cd[m] * (1.0 / pd), 0.0)
            for n in range(m + 1, 8):
                cu[n] = cu[n] - fu * cu[n][k:k + 1, :]
                cd[n] = cd[n] - fd * cd[n][k:k + 1, :]
            a1 = a1 - jnp.where(in_dn, fd, fu) * a1[k:k + 1, :]
            a2 = a2 - fd * a2[k:k + 1, :]
            scale_u = jnp.where(row == k, lax.rsqrt(pu), scale_u)
            scale_d = jnp.where(row == k, lax.rsqrt(pd), scale_d)
    return a1 * scale_u, a2 * scale_d


def exchange(ug, ue, uw, dg, de, dw, fa_out, fb_out, wu_out, wd_out,
             vug, vue, vuw, vdg, vde, vdw, TU, TD, CU, CD, XU, YD, YU, XD, FA, FB,
             pt, pc, px, pxr, pz, py, pg,
             in_sem, s_cu, r_cu, s_cd, r_cd, s_xu, r_xu, s_yd, r_yd, s_yu, r_yu, s_xd, r_xd,
             s_pc, r_pc, s_px, r_px, s_pz, r_pz, s_py, r_py, s_pa, r_pa, s_pb, r_pb,
             s_ay, r_ay, s_ax, r_ax, s_ac, r_ac, s_bx, r_bx, s_by, r_by, s_bc, r_bc, out_sem):
    d = lax.axis_index("dp")
    z = lax.axis_index("mp")
    c = lax.rem(d, 2)
    x = lax.rem(lax.div(d, 2), NX)
    y = lax.div(d, 8)
    other = 1 - c

    def at(yy, xx, cc):
        return ((yy * NX + xx) * NC + cc, z)

    partner = at(y, x, other)

    def xpeer(o):
        return at(y, lax.rem(x + o, NX), c)

    def ypeer(o):
        return at(lax.rem(y + o, NY), x, c)

    def zpeer(o):
        return (d, lax.rem(z + o, NZ))

    bar = pltpu.get_barrier_semaphore()
    for o in (4, 3, 5, 2, 6, 1, 7):
        pl.semaphore_signal(bar, 1, device_id=zpeer(o), device_id_type=MESH)
        pl.semaphore_signal(bar, 1, device_id=ypeer(o), device_id_type=MESH)
    for o in (2, 1, 3):
        pl.semaphore_signal(bar, 1, device_id=xpeer(o), device_id_type=MESH)
    pl.semaphore_signal(bar, 1, device_id=partner, device_id_type=MESH)

    loads = [pltpu.make_async_copy(a, b, in_sem.at[i])
             for i, (a, b) in enumerate([(dg, vdg), (de, vde), (dw, vdw), (ug, vug), (ue, vue), (uw, vuw)])]
    for cp in loads:
        cp.start()

    def down_part(b):
        cols = pl.ds(256 * b, 256)
        return vdg[:, cols].astype(F32) + vde[:, cols]

    def up_part(half, b):
        cols = pl.ds(half * HALF + 256 * b, 256)
        return vug[:, cols].astype(F32) + vue[:, cols]

    for cp in loads[:3]:
        cp.wait()
    acc = jnp.zeros((RANK, DN_R), F32)
    for b in range(DN_C // 256):
        acc += nt3(vdw[:, pl.ds(256 * b, 256)], down_part(b))
    pt[32:64, :] = acc
    for cp in loads[3:]:
        cp.wait()
    acc = jnp.zeros((RANK, UP_R), F32)
    for b in range(HALF // 256):
        for half in range(2):
            acc += nt3(vuw[:, pl.ds(half * HALF + 256 * b, 256)], up_part(half, b))
    pt[0:32, :] = jnp.concatenate([acc, jnp.zeros((RANK, 64), F32)], axis=1)

    pl.semaphore_wait(bar, 1 + 7 + 7 + 3)

    sent = []

    def remote(src, dst, ssem, rsem, dev):
        cp = pltpu.make_async_remote_copy(src_ref=src, dst_ref=dst, send_sem=ssem, recv_sem=rsem,
                                          device_id=dev, device_id_type=MESH)
        cp.start()
        sent.append(cp)
        return cp

    cp_pc = remote(pt.at[pl.ds(pl.multiple_of(other * 32, 32), 32)], pc, s_pc, r_pc, partner)

    for b in range(HALF // 256):
        stacked = jnp.concatenate([up_part(0, b), up_part(1, b)], axis=0)
        for s in range(2):
            turned = stacked[:, 128 * s:128 * (s + 1)].T
            for i in range(16):
                tile = (2 * b + s) * 16 + i
                q, u = tile // 7, tile % 7
                rows = turned[8 * i:8 * i + 8, :]
                if u <= 3:
                    TU[0, q // NY, q % NY, 8 * u:8 * u + 8, :] = rows
                if u >= 3:
                    TU[1, q // NY, q % NY, 8 * (u - 3):8 * (u - 3) + 8, :] = rows

    cp_pc.wait_recv()
    px[...] = pt[pl.ds(pl.multiple_of(c * 32, 32), 32), :] + pc[...]
    cp_px = [remote(px.at[pl.ds(pl.multiple_of(lax.rem(x + o, NX) * 8, 8), 8)], pxr.at[o - 1],
                    s_px.at[o - 1], r_px.at[o - 1], xpeer(o)) for o in (2, 1, 3)]

    for b in range(DN_C // 256):
        m = down_part(b)
        for s in range(2):
            turned = m[:, 128 * s:128 * (s + 1)].T
            for i in range(16):
                tile = (2 * b + s) * 16 + i
                q, u = tile // 4, tile % 4
                TD[u // 2, q % NY, q // NY, 8 * (u % 2):8 * (u % 2) + 8, :] = turned[8 * i:8 * i + 8, :]

    order = [(0, 2), (1, 4), (1, 3), (1, 5), (0, 1), (1, 2), (1, 6), (0, 3), (1, 1), (1, 7), (0, 0), (1, 0)]
    cp_c = {}
    for kind, o in order:
        if kind == 0:
            xx = lax.rem(x + o, NX)
            cp_c[kind, o] = remote(TU.at[other, xx], CU.at[xx], s_cu.at[o], r_cu.at[o], partner)
        else:
            yy = lax.rem(y + o, NY)
            cp_c[kind, o] = remote(TD.at[other, yy], CD.at[yy], s_cd.at[o], r_cd.at[o], partner)
    cp_xu, cp_yd = [], []
    for kind, o in order:
        cp_c[kind, o].wait_recv()
        if kind == 0:
            xx = lax.rem(x + o, NX)
            TU[c, xx] = TU[c, xx] + CU[xx]
            if o:
                cp_xu.append(remote(TU.at[c, xx], XU.at[o - 1], s_xu.at[o - 1], r_xu.at[o - 1], xpeer(o)))
        else:
            yy = lax.rem(y + o, NY)
            TD[c, yy] = TD[c, yy] + CD[yy]
            if o:
                cp_yd.append(remote(TD.at[c, yy], YD.at[o - 1], s_yd.at[o - 1], r_yd.at[o - 1], ypeer(o)))

    for cp in cp_px:
        cp.wait_recv()
    mine = pl.ds(pl.multiple_of(x * 8, 8), 8)
    pz[z] = (px[mine, :] + pxr[0]) + (pxr[1] + pxr[2])
    cp_pz = [remote(pz.at[z], pz.at[z], s_pz.at[o - 1], r_pz.at[o - 1], zpeer(o)) for o in (4, 3, 5, 2, 6, 1, 7)]
    for cp in cp_pz:
        cp.wait_recv()
    py[y] = ((pz[0] + pz[1]) + (pz[2] + pz[3])) + ((pz[4] + pz[5]) + (pz[6] + pz[7]))
    cp_py = [remote(py.at[y], py.at[y], s_py.at[o - 1], r_py.at[o - 1], ypeer(o)) for o in (4, 3, 5, 2, 6, 1, 7)]

    for cp in cp_xu:
        cp.wait_recv()
    cp_yu = []
    for o in (4, 3, 5, 2, 6, 1, 7, 0):
        yy = lax.rem(y + o, NY)
        TU[c, x, yy] = (TU[c, x, yy] + XU[0, yy]) + (XU[1, yy] + XU[2, yy])
        if o:
            cp_yu.append(remote(TU.at[c, x, yy], YU.at[o - 1], s_yu.at[o - 1], r_yu.at[o - 1], ypeer(o)))

    for cp in cp_py:
        cp.wait_recv()
    pg[c, mine, :] = ((py[0] + py[1]) + (py[2] + py[3])) + ((py[4] + py[5]) + (py[6] + py[7]))
    cp_pa = [remote(pg.at[c, mine], pg.at[c, mine], s_pa.at[o - 1], r_pa.at[o - 1], xpeer(o)) for o in (2, 1, 3)]

    for cp in cp_yd:
        cp.wait_recv()
    cp_xd = []
    for o in (2, 1, 3, 0):
        xx = lax.rem(x + o, NX)
        tot = TD[c, y, xx]
        for i in range(NY - 1):
            tot = tot + YD[i, xx]
        TD[c, y, xx] = tot
        if o:
            cp_xd.append(remote(TD.at[c, y, xx], XD.at[o - 1], s_xd.at[o - 1], r_xd.at[o - 1], xpeer(o)))

    for cp in cp_pa:
        cp.wait_recv()
    cp_pb = remote(pg.at[c], pg.at[c], s_pb, r_pb, partner)
    cp_pb.wait_recv()

    a1 = pg[0]
    a2 = pg[1]
    gu = nt(a1, a1, HI)
    gd = nt(a2, a2, HI)
    a1, a2 = eliminate(jnp.concatenate([a1[:, :64], gu, gd], axis=1), a2)
    lane = lax.broadcasted_iota(jnp.int32, (RANK, 128), 1)
    left = jnp.where(lane < 64, a1, 0.0)
    right = pltpu.roll(left, 64, axis=1)
    wu = jnp.concatenate([left, right, left, right], axis=0)
    wd = jnp.concatenate([a2, a2, a2, a2], axis=0)

    lane16 = lax.broadcasted_iota(jnp.int32, (16, 128), 1)
    for cp in cp_xd:
        cp.wait_recv()
    shard = ((TD[c, y, x] + XD[0]) + (XD[1] + XD[2])) * (1.0 / 64.0)
    rd = nt(shard, wd, HI)
    FB[c, y, x] = jnp.where(lane16[0:8] < 32, rd[0:8], rd[8:16])
    cp_bx = [remote(FB.at[c, y, x], FB.at[c, y, x], s_bx.at[o - 1], r_bx.at[o - 1], xpeer(o)) for o in (2, 1, 3)]
    for cp in cp_yu:
        cp.wait_recv()
    shard = TU[c, x, y]
    for i in range(NY - 1):
        shard = shard + YU[i]
    ru = nt(shard * (1.0 / 64.0), wu, HI)
    FA[c, x, y] = jnp.where(lane16 < 64, ru[0:16], ru[16:32])
    cp_ay = [remote(FA.at[c, x, y], FA.at[c, x, y], s_ay.at[o - 1], r_ay.at[o - 1], ypeer(o)) for o in (4, 3, 5, 2, 6, 1, 7)]
    wu_out[...] = wu.T
    wd_out[...] = wd.T
    for cp in cp_bx:
        cp.wait_recv()
    yo = (4, 3, 5, 2, 6, 1, 7)
    cp_by = [remote(FB.at[c, y], FB.at[c, y], s_by.at[o - 1], r_by.at[o - 1], ypeer(o)) for o in yo]
    cp_bc = [remote(FB.at[c, y], FB.at[c, y], s_bc.at[0], r_bc.at[0], partner)]
    for cp in cp_ay:
        cp.wait_recv()
    cp_ax = [remote(FA.at[c, x], FA.at[c, x], s_ax.at[o - 1], r_ax.at[o - 1], xpeer(o)) for o in (2, 1, 3)]
    cp_ac = [remote(FA.at[c, x], FA.at[c, x], s_ac.at[0], r_ac.at[0], partner)]
    for cp, o in zip(cp_by, yo):
        cp.wait_recv()
        yy = lax.rem(y - o + NY, NY)
        cp_bc.append(remote(FB.at[c, yy], FB.at[c, yy], s_bc.at[o], r_bc.at[o], partner))
    for cp, o in zip(cp_ax, (2, 1, 3)):
        cp.wait_recv()
        xx = lax.rem(x - o + NX, NX)
        cp_ac.append(remote(FA.at[c, xx], FA.at[c, xx], s_ac.at[o], r_ac.at[o], partner))
    outs = [pltpu.make_async_copy(FA.at[c], fa_out.at[c], out_sem.at[0]),
            pltpu.make_async_copy(FB.at[c], fb_out.at[c], out_sem.at[1])]
    for cp in outs:
        cp.start()
    for cp in cp_bc:
        cp.wait_recv()
    outs.append(pltpu.make_async_copy(FB.at[other], fb_out.at[other], out_sem.at[3]))
    outs[-1].start()
    for cp in cp_ac:
        cp.wait_recv()
    outs.append(pltpu.make_async_copy(FA.at[other], fa_out.at[other], out_sem.at[2]))
    outs[-1].start()
    for cp in sent:
        cp.wait_send()
    for cp in outs:
        cp.wait()


def finish(fa, fb, wu, wd, ug, ue, dg, de, ua, ur, da, dr, fu, fd):
    lane = lax.broadcasted_iota(jnp.int32, (8, 128), 1)
    for tile in range(HALF // 8):
        q, u = tile // 7, tile % 7
        core, s = (0, u) if u <= 3 else (1, u - 3)
        r0 = (s % 2) * 8
        rows = fa[core, q // NY, q % NY, r0:r0 + 8, :]
        fu[8 * tile:8 * tile + 8, :] = jnp.where(lane // 64 == s // 2, rows, 0.0)
    for tile in range(DN_C // 8):
        q, u = tile // 4, tile % 4
        rows = fb[u // 2, q % NY, q // NY]
        fd[8 * tile:8 * tile + 8, :] = jnp.where(lane // 32 == u % 2, rows, 0.0)
    for b in range(HALF // 256):
        delta = nt3(wu[...], fu[256 * b:256 * b + 256, :])
        for half in range(2):
            cols = pl.ds(half * HALF + 256 * b, 256)
            part = delta[64 * half:64 * half + 64, :]
            ua[:, cols] = part.astype(BF16)
            ur[:, cols] = (ug[:, cols].astype(F32) + ue[:, cols]) - part
    for b in range(DN_C // 256):
        cols = pl.ds(256 * b, 256)
        delta = nt3(wd[...], fd[256 * b:256 * b + 256, :])
        da[:, cols] = delta.astype(BF16)
        dr[:, cols] = (dg[:, cols].astype(F32) + de[:, cols]) - delta


def body(up_grad, up_error, up_warm, down_grad, down_error, down_warm):
    ug, ue, dg, de = up_grad[0], up_error[0], down_grad[0], down_error[0]
    vm = pl.BlockSpec(memory_space=pltpu.VMEM)
    hbm = pl.BlockSpec(memory_space=pltpu.HBM)
    dma = pltpu.SemaphoreType.DMA
    V = pltpu.VMEM
    fa, fb, wu, wd = pl.pallas_call(
        exchange,
        out_shape=(
            jax.ShapeDtypeStruct((NC, NX, NY, 16, 128), F32),
            jax.ShapeDtypeStruct((NC, NY, NX, 8, 128), F32),
            jax.ShapeDtypeStruct((128, 128), F32),
            jax.ShapeDtypeStruct((128, 128), F32),
        ),
        in_specs=[hbm] * 6,
        out_specs=(pl.BlockSpec(memory_space=pl.ANY),) * 2 + (vm, vm),
        scratch_shapes=[
            V((UP_R, UP_C), BF16), V((UP_R, UP_C), F32), V((RANK, UP_C), F32),
            V((DN_R, DN_C), BF16), V((DN_R, DN_C), F32), V((RANK, DN_C), F32),
            V((NC, NX, NY, 32, 128), F32), V((NC, NY, NX, 16, 128), F32),
            V((NX, NY, 32, 128), F32), V((NY, NX, 16, 128), F32),
            V((NX - 1, NY, 32, 128), F32), V((NY - 1, NX, 16, 128), F32),
            V((NY - 1, 32, 128), F32), V((NX - 1, 16, 128), F32),
            V((NC, NX, NY, 16, 128), F32), V((NC, NY, NX, 8, 128), F32),
            V((64, 128), F32), V((32, 128), F32), V((32, 128), F32), V((3, 8, 128), F32),
            V((NZ, 8, 128), F32), V((NY, 8, 128), F32), V((2, 32, 128), F32),
            dma((6,)), *[dma((n,)) for n in (4, 4, 8, 8, 3, 3, 7, 7, 7, 7, 3, 3)],
            dma, dma, dma((3,)), dma((3,)), dma((7,)), dma((7,)), dma((7,)), dma((7,)), dma((3,)), dma((3,)), dma, dma,
            *[dma((n,)) for n in (7, 7, 3, 3, 4, 4, 3, 3, 7, 7, 8, 8)], dma((4,)),
        ],
        compiler_params=pltpu.CompilerParams(
            collective_id=0, has_side_effects=True, vmem_limit_bytes=32 * 1024 * 1024),
        name="exchange",
    )(*[pltpu.with_memory_space_constraint(a, pltpu.HBM) for a in (ug, ue, up_warm.T, dg, de, down_warm.T)])
    ua, ur, da, dr = pl.pallas_call(
        finish,
        out_shape=(
            jax.ShapeDtypeStruct((UP_R, UP_C), BF16),
            jax.ShapeDtypeStruct((UP_R, UP_C), F32),
            jax.ShapeDtypeStruct((DN_R, DN_C), BF16),
            jax.ShapeDtypeStruct((DN_R, DN_C), F32),
        ),
        in_specs=[vm] * 8,
        out_specs=(vm,) * 4,
        scratch_shapes=[V((HALF, 128), F32), V((DN_C, 128), F32)],
        compiler_params=pltpu.CompilerParams(vmem_limit_bytes=32 * 1024 * 1024),
        name="finish",
    )(fa, fb, wu, wd, ug, ue, dg, de)
    return ua, ur[None], da, dr[None]


def solution(mesh):
    return jax.shard_map(
        body,
        mesh=mesh,
        in_specs=(
            P("dp", None, "mp"),
            P("dp", None, "mp"),
            P("mp", None),
            P("dp", None, "mp"),
            P("dp", None, "mp"),
            P("mp", None),
        ),
        out_specs=(P(None, "mp"), P("dp", None, "mp"), P(None, "mp"), P("dp", None, "mp")),
        check_vma=False,
    )
```

```python
import jax
import jax.numpy as jnp
from jax import lax
from jax.experimental import pallas as pl
from jax.experimental.pallas import tpu as pltpu
from jax.sharding import PartitionSpec as P

F32 = jnp.float32
BF16 = jnp.bfloat16
HI = lax.Precision.HIGHEST
MESH = pl.DeviceIdType.MESH
NY, NX, NC, NZ = 8, 4, 2, 8
RANK = 32
UP_R, UP_C = 64, 3584
DN_R, DN_C = 128, 1024
HALF = UP_C // 2


def nt(a, b, precision=None):
    return lax.dot_general(a, b, (((1,), (1,)), ((), ())), preferred_element_type=F32, precision=precision)


def split(a):
    hi = a.astype(BF16)
    return hi, (a - hi.astype(F32)).astype(BF16)


def nt3(a, b):
    ah, al = split(a)
    bh, bl = split(b)
    return nt(ah, bh) + nt(ah, bl) + nt(al, bh)


def eliminate(arrays, where, off):
    shape = (RANK, 128)
    row = lax.broadcasted_iota(jnp.int32, shape, 0)
    scale = jnp.ones(shape, F32)
    for first in range(0, RANK, 8):
        cols = [jnp.broadcast_to(arrays[where][:, off + first + m:off + first + m + 1], shape) for m in range(8)]
        for m in range(8):
            k = first + m
            pivot = cols[m][k:k + 1, :]
            factor = jnp.where(row > k, cols[m] * (1.0 / pivot), 0.0)
            for n in range(m + 1, 8):
                cols[n] = cols[n] - factor * cols[n][k:k + 1, :]
            arrays = [a - factor * a[k:k + 1, :] for a in arrays]
            scale = jnp.where(row == k, lax.rsqrt(pivot), scale)
    return arrays[0] * scale


def exchange(ug, ue, uw, dg, de, dw, FA0, FA1, FB, wu_out, wd_out,
             vug, vue, vuw, vdg, vde, vdw, TU0, TU1, TD0, TD1, CU0, CU1, CD, XU0, XU1, YD, YU0, YU1, XD0, XD1,
             SA0, SA1, SB, SW, pt, pc, px, pxr, pz, py, pg,
             in_sem, s_cu, r_cu, s_cd, r_cd, s_xu, r_xu, s_yd, r_yd, s_yu, r_yu, s_xd, r_xd, s_vu, r_vu, s_vd, r_vd,
             s_px, r_px, s_pz, r_pz, s_py, r_py, s_pa, r_pa,
             s_ay, r_ay, s_a1, r_a1, s_ax, r_ax, s_ac, r_ac, s_ad, r_ad, s_bx, r_bx, s_by, r_by, s_bc, r_bc, own_sem,
             s_pc, r_pc, s_wu, r_wu, s_wd, r_wd):
    d = lax.axis_index("dp")
    z = lax.axis_index("mp")
    c = lax.rem(d, 2)
    x = lax.rem(lax.div(d, 2), NX)
    y = lax.div(d, 8)
    other = 1 - c
    far_y = (4, 3, 5, 2, 6, 1, 7)
    far_x = (2, 1, 3)

    def at(yy, xx, cc):
        return ((yy * NX + xx) * NC + cc, z)

    partner = at(y, x, other)

    xs = [lax.rem(x + o, NX) for o in range(NX)]
    ys = [lax.rem(y + o, NY) for o in range(NY)]
    zs = [lax.rem(z + o, NZ) for o in range(NZ)]

    def xof(o):
        return xs[o % NX]

    def yof(o):
        return ys[o % NY]

    def xpeer(o):
        return at(y, xof(o), c)

    def ypeer(o):
        return at(yof(o), x, c)

    def zpeer(o):
        return (d, zs[o])

    pairs = []
    for half in range(2):
        cols = pl.ds(half * HALF, HALF)
        pairs += [(ug.at[:, cols], vug.at[:, cols]), (ue.at[:, cols], vue.at[:, cols]), (uw.at[:, cols], vuw.at[:, cols])]
    pairs += [(dg, vdg), (de, vde), (dw, vdw)]
    loads = [pltpu.make_async_copy(a, b, in_sem.at[i]) for i, (a, b) in enumerate(pairs)]
    for cp in loads:
        cp.start()

    bar = pltpu.get_barrier_semaphore()
    for o in far_y:
        pl.semaphore_signal(bar, 1, device_id=zpeer(o), device_id_type=MESH)
        pl.semaphore_signal(bar, 1, device_id=ypeer(o), device_id_type=MESH)
    for o in far_x:
        pl.semaphore_signal(bar, 1, device_id=xpeer(o), device_id_type=MESH)
    pl.semaphore_signal(bar, 1, device_id=partner, device_id_type=MESH)

    def down_part(b):
        cols = pl.ds(256 * b, 256)
        return vdg[:, cols].astype(F32) + vde[:, cols]

    def up_part(half, b):
        cols = pl.ds(half * HALF + 256 * b, 256)
        return vug[:, cols].astype(F32) + vue[:, cols]

    acc = jnp.zeros((RANK, UP_R), F32)
    for half in range(2):
        for cp in loads[3 * half:3 * half + 3]:
            cp.wait()
        for b in range(HALF // 256):
            acc += nt3(vuw[:, pl.ds(half * HALF + 256 * b, 256)], up_part(half, b))
    pt[0:32, :] = jnp.concatenate([acc, jnp.zeros((RANK, 64), F32)], axis=1)
    for cp in loads[6:]:
        cp.wait()
    acc = jnp.zeros((RANK, DN_R), F32)
    for b in range(DN_C // 256):
        acc += nt3(vdw[:, pl.ds(256 * b, 256)], down_part(b))
    pt[32:64, :] = acc

    pl.semaphore_wait(bar, 1 + 7 + 7 + 3)

    def describe(src, dst, ssem, rsem, dev):
        return pltpu.make_async_remote_copy(src_ref=src, dst_ref=dst, send_sem=ssem, recv_sem=rsem,
                                            device_id=dev, device_id_type=MESH)

    def remote(log, src, dst, ssem, rsem, dev):
        cp = describe(src, dst, ssem, rsem, dev)
        cp.start()
        log.append(cp)
        return cp

    sent = []
    cp_pc = remote(sent, pt.at[pl.ds(pl.multiple_of(other * 32, 32), 32)], pc, s_pc, r_pc, partner)

    for b in range(HALF // 256):
        stacked = jnp.concatenate([up_part(0, b), up_part(1, b)], axis=0)
        for s in range(2):
            turned = stacked[:, 128 * s:128 * (s + 1)].T
            for i in range(16):
                tile = (2 * b + s) * 16 + i
                q, u = tile // 7, tile % 7
                dst, r0 = (TU0, 8 * u) if u < 4 else (TU1, 8 * u - 32)
                dst[q // NY, q % NY, r0:r0 + 8, :] = turned[8 * i:8 * i + 8, :]

    cp_pc.wait_recv()
    px[...] = pt[pl.ds(pl.multiple_of(c * 32, 32), 32), :] + pc[...]
    cp_px = [remote(sent, px.at[pl.ds(pl.multiple_of(xof(o) * 8, 8), 8)], pxr.at[o - 1],
                    s_px.at[o - 1], r_px.at[o - 1], xpeer(o)) for o in far_x]

    for b in range(DN_C // 256):
        m = down_part(b)
        for s in range(2):
            turned = m[:, 128 * s:128 * (s + 1)].T
            for i in range(4):
                q = (2 * b + s) * 4 + i
                TD0[q // NX, q % NX] = turned[32 * i:32 * i + 16, :]
                TD1[q // NX, q % NX] = turned[32 * i + 16:32 * i + 32, :]

    mine = pl.ds(pl.multiple_of(x * 8, 8), 8)

    def proj_z(log):
        for cp in cp_px:
            cp.wait_recv()
        pz[z] = (px[mine, :] + pxr[0]) + (pxr[1] + pxr[2])
        return [remote(log, pz.at[z], pz.at[z], s_pz.at[o - 1], r_pz.at[o - 1], zpeer(o)) for o in far_y]

    def proj_y(log, cps):
        for cp in cps:
            cp.wait_recv()
        py[y] = ((pz[0] + pz[1]) + (pz[2] + pz[3])) + ((pz[4] + pz[5]) + (pz[6] + pz[7]))
        return [remote(log, py.at[y], py.at[y], s_py.at[o - 1], r_py.at[o - 1], ypeer(o)) for o in far_y]

    def proj_x(log, cps):
        for cp in cps:
            cp.wait_recv()
        pg[mine, :] = ((py[0] + py[1]) + (py[2] + py[3])) + ((py[4] + py[5]) + (py[6] + py[7]))
        return [remote(log, pg.at[mine], pg.at[mine], s_pa.at[o - 1], r_pa.at[o - 1], xpeer(o)) for o in far_x]

    lane = lax.broadcasted_iota(jnp.int32, (RANK, 128), 1)
    lane16 = lane[0:16]
    lane8 = lane[0:8]

    def local(log, src, dst, sem):
        cp = pltpu.make_async_copy(src, dst, sem)
        cp.start()
        log.append(cp)
        return cp

    def sum_merged(core, log):
        tu, tu_other = (TU0, TU1) if core == 0 else (TU1, TU0)
        td, td_other = (TD0, TD1) if core == 0 else (TD1, TD0)
        cu, cu_other = (CU0, CU1) if core == 0 else (CU1, CU0)
        xu = XU0 if core == 0 else XU1
        order = [(0, 2), (1, 4), (1, 3), (1, 5), (0, 1), (1, 2), (1, 6), (0, 3), (1, 1), (1, 7), (0, 0), (1, 0)]
        for kind, o in order:
            if kind == 0:
                remote(log, tu_other.at[xs[o]], cu_other.at[xs[o]], s_cu.at[o], r_cu.at[o], partner)
            else:
                remote(log, td_other.at[ys[o]], CD.at[ys[o]], s_cd.at[o], r_cd.at[o], partner)
        cp_xu, cp_yd = [], []
        for kind, o in order:
            if kind == 0:
                xx = xs[o]
                describe(tu.at[xx], cu.at[xx], s_cu.at[o], r_cu.at[o], partner).wait_recv()
                tu[xx] = tu[xx] + cu[xx]
                if o:
                    cp_xu.append(remote(log, tu.at[xx], xu.at[o - 1], s_xu.at[o - 1], r_xu.at[o - 1], xpeer(o)))
            else:
                yy = ys[o]
                describe(td.at[yy], CD.at[yy], s_cd.at[o], r_cd.at[o], partner).wait_recv()
                td[yy] = td[yy] + CD[yy]
                if o:
                    cp_yd.append(remote(log, td.at[yy], YD.at[o - 1], s_yd.at[o - 1], r_yd.at[o - 1], ypeer(o)))

        cp_py = proj_y(log, proj_z(log))

        for cp in cp_xu:
            cp.wait_recv()
        for o in far_y + (0,):
            yy = ys[o]
            tu[x, yy] = (tu[x, yy] + xu[0, yy]) + (xu[1, yy] + xu[2, yy])
            if core == 1:
                remote(log, tu.at[x, yy], YU1.at[o], s_vu.at[o], r_vu.at[o], at(yy, x, 0))
            elif o:
                remote(log, tu.at[x, yy], YU0.at[o - 1], s_yu.at[o - 1], r_yu.at[o - 1], at(yy, x, 0))

        cp_pa = proj_x(log, cp_py)

        for cp in cp_yd:
            cp.wait_recv()
        for o in far_x + (0,):
            xx = xs[o]
            tot = td[y, xx]
            for i in range(NY - 1):
                tot = tot + YD[i, xx]
            td[y, xx] = tot
            if core == 0:
                remote(log, td.at[y, xx], XD0.at[o], s_vd.at[o], r_vd.at[o], at(y, xx, 1))
            elif o:
                remote(log, td.at[y, xx], XD1.at[o - 1], s_xd.at[o - 1], r_xd.at[o - 1], at(y, xx, 1))
        for cp in cp_pa:
            cp.wait_recv()

    @pl.when(c == 0)
    def _():
        log, near = [], []
        sum_merged(0, log)
        a = pg[...]
        gram = nt(a, a, HI)
        a = eliminate([jnp.concatenate([a[:, :64], gram, jnp.zeros((RANK, 32), F32)], axis=1)], 0, 64)
        left = jnp.where(lane < 64, a, 0.0)
        right = pltpu.roll(left, 64, axis=1)
        w = jnp.concatenate([left, right, left, right], axis=0)
        for o in far_y:
            describe(TU0.at[x, y], YU0.at[o - 1], s_yu.at[o - 1], r_yu.at[o - 1], partner).wait_recv()
        for o in far_y + (0,):
            describe(TU1.at[x, y], YU1.at[o], s_vu.at[o], r_vu.at[o], partner).wait_recv()
        low = TU0[x, y]
        for i in range(NY - 1):
            low = low + YU0[i]
        high = YU1[0]
        for i in range(1, NY):
            high = high + YU1[i]
        r = nt(jnp.concatenate([low, high], axis=0) * (1.0 / 64.0), w, HI)
        SA1[...] = jnp.where(lane16 < 64, r[16:32], jnp.concatenate([r[48:56], jnp.zeros((8, 128), F32)], axis=0))
        SA0[...] = jnp.where(lane16 < 64, r[0:16], r[32:48])

        cp_ay = []
        for o in far_y:
            remote(log, SA1, FA1.at[x, y], s_a1.at[o], r_a1.at[o], at(ys[o], x, 1))
            cp_ay.append(remote(log, SA0, FA0.at[x, y], s_ay.at[o - 1], r_ay.at[o - 1], ypeer(o)))
        remote(log, SA1, FA1.at[x, y], s_a1.at[0], r_a1.at[0], partner)
        local(near, SA0, FA0.at[x, y], own_sem.at[0])
        SW[...] = w.T
        remote(log, SW, wu_out, s_wu, r_wu, partner)
        local(near, SW, wu_out, own_sem.at[1])
        near[0].wait()
        for cp in cp_ay:
            cp.wait_recv()
        cp_ax = [remote(log, FA0.at[x], FA0.at[x], s_ax.at[o - 1], r_ax.at[o - 1], xpeer(o)) for o in far_x]
        remote(log, FA0.at[x], FA0.at[x], s_ac.at[0], r_ac.at[0], partner)
        for cp, o in zip(cp_ax, far_x):
            cp.wait_recv()
            xx = xof(NX - o)
            remote(log, FA0.at[xx], FA0.at[xx], s_ac.at[o], r_ac.at[o], partner)
        describe(SW, wd_out, s_wd, r_wd, partner).wait_recv()
        for o in range(NY):
            describe(FB.at[ys[o]], FB.at[ys[o]], s_bc.at[o], r_bc.at[o], partner).wait_recv()
        for o in range(NX):
            describe(FA1.at[xs[o]], FA1.at[xs[o]], s_ad.at[o], r_ad.at[o], partner).wait_recv()
        for cp in log:
            cp.wait_send()
        near[1].wait()

    @pl.when(c == 1)
    def _():
        log, near = [], []
        sum_merged(1, log)
        a = pg[...]
        gram = nt(a, a, HI)
        a = eliminate([a, jnp.concatenate([gram, jnp.zeros((RANK, 96), F32)], axis=1)], 1, 0)
        w = jnp.concatenate([a, a, a, a], axis=0)
        for o in far_x:
            describe(TD1.at[y, x], XD1.at[o - 1], s_xd.at[o - 1], r_xd.at[o - 1], partner).wait_recv()
        for o in far_x + (0,):
            describe(TD0.at[y, x], XD0.at[o], s_vd.at[o], r_vd.at[o], partner).wait_recv()
        low = (XD0[0] + XD0[1]) + (XD0[2] + XD0[3])
        high = (TD1[y, x] + XD1[0]) + (XD1[1] + XD1[2])
        r = nt(jnp.concatenate([low, high], axis=0) * (1.0 / 64.0), w, HI)
        low = jnp.where(lane8 < 32, r[0:8], r[8:16])
        high = jnp.where(lane8 < 96, r[16:24], r[24:32])
        SB[...] = jnp.where(lane8 < 64, low, high)

        cp_bx = [remote(log, SB, FB.at[y, x], s_bx.at[o - 1], r_bx.at[o - 1], xpeer(o)) for o in far_x]
        local(near, SB, FB.at[y, x], own_sem.at[0])
        SW[...] = w.T
        remote(log, SW, wd_out, s_wd, r_wd, partner)
        local(near, SW, wd_out, own_sem.at[1])
        near[0].wait()
        for cp in cp_bx:
            cp.wait_recv()
        cp_by = [remote(log, FB.at[y], FB.at[y], s_by.at[o - 1], r_by.at[o - 1], ypeer(o)) for o in far_y]
        remote(log, FB.at[y], FB.at[y], s_bc.at[0], r_bc.at[0], partner)
        for o in (0,) + far_y:
            describe(SA1, FA1.at[x, yof(NY - o)], s_a1.at[o], r_a1.at[o], partner).wait_recv()
        cp_ax = [remote(log, FA1.at[x], FA1.at[x], s_ax.at[o - 1], r_ax.at[o - 1], xpeer(o)) for o in far_x]
        remote(log, FA1.at[x], FA1.at[x], s_ad.at[0], r_ad.at[0], partner)
        for cp, o in zip(cp_by, far_y):
            cp.wait_recv()
            yy = yof(NY - o)
            remote(log, FB.at[yy], FB.at[yy], s_bc.at[o], r_bc.at[o], partner)
        for cp, o in zip(cp_ax, far_x):
            cp.wait_recv()
            xx = xof(NX - o)
            remote(log, FA1.at[xx], FA1.at[xx], s_ad.at[o], r_ad.at[o], partner)
        describe(SW, wu_out, s_wu, r_wu, partner).wait_recv()
        for o in range(NX):
            describe(FA0.at[xs[o]], FA0.at[xs[o]], s_ac.at[o], r_ac.at[o], partner).wait_recv()
        for cp in log:
            cp.wait_send()
        near[1].wait()

    for cp in sent:
        cp.wait_send()


def finish(fa0, fa1, fb, wu, wd, ug, ue, dg, de, ua, ur, da, dr, bua, bur, bda, bdr, sem):
    lane = lax.broadcasted_iota(jnp.int32, (8, 128), 1)
    started = []

    def store(src, dst, cols):
        cp = pltpu.make_async_copy(src.at[:, cols], dst.at[:, cols], sem.at[len(started)])
        cp.start()
        started.append(cp)

    def up_tile(tile):
        q, u = tile // 7, tile % 7
        src, r0 = (fa0, fa1)[u % 4 // 2], (u % 2) * 8
        return jnp.where(lane // 64 == u // 4, src[q // NY, q % NY, r0:r0 + 8, :], 0.0)

    def down_tile(tile):
        q, u = tile // 4, tile % 4
        return jnp.where(lane // 32 == u, fb[q // NX, q % NX], 0.0)

    for first, last in ((0, 2), (2, 4), (4, 6), (6, 7)):
        for b in range(first, last):
            delta = nt3(wu[...], jnp.concatenate([up_tile(32 * b + i) for i in range(32)], axis=0))
            for half in range(2):
                cols = pl.ds(half * HALF + 256 * b, 256)
                part = delta[64 * half:64 * half + 64, :]
                bua[:, cols] = part.astype(BF16)
                bur[:, cols] = (ug[:, cols].astype(F32) + ue[:, cols]) - part
        for half in range(2):
            cols = pl.ds(half * HALF + 256 * first, 256 * (last - first))
            store(bua, ua, cols)
            store(bur, ur, cols)
    for first, last in ((0, 2), (2, 4)):
        for b in range(first, last):
            cols = pl.ds(256 * b, 256)
            delta = nt3(wd[...], jnp.concatenate([down_tile(32 * b + i) for i in range(32)], axis=0))
            bda[:, cols] = delta.astype(BF16)
            bdr[:, cols] = (dg[:, cols].astype(F32) + de[:, cols]) - delta
        cols = pl.ds(256 * first, 256 * (last - first))
        store(bda, da, cols)
        store(bdr, dr, cols)
    for cp in started:
        cp.wait()


def body(up_grad, up_error, up_warm, down_grad, down_error, down_warm):
    ug, ue, dg, de = up_grad[0], up_error[0], down_grad[0], down_error[0]
    vm = pl.BlockSpec(memory_space=pltpu.VMEM)
    hbm = pl.BlockSpec(memory_space=pltpu.HBM)
    anywhere = pl.BlockSpec(memory_space=pl.ANY)
    dma = pltpu.SemaphoreType.DMA
    V = pltpu.VMEM
    fa0, fa1, fb, wu, wd = pl.pallas_call(
        exchange,
        out_shape=(
            jax.ShapeDtypeStruct((NX, NY, 16, 128), F32),
            jax.ShapeDtypeStruct((NX, NY, 16, 128), F32),
            jax.ShapeDtypeStruct((NY, NX, 8, 128), F32),
            jax.ShapeDtypeStruct((128, 128), F32),
            jax.ShapeDtypeStruct((128, 128), F32),
        ),
        in_specs=[hbm] * 6,
        out_specs=(anywhere,) * 5,
        scratch_shapes=[
            V((UP_R, UP_C), BF16), V((UP_R, UP_C), F32), V((RANK, UP_C), F32),
            V((DN_R, DN_C), BF16), V((DN_R, DN_C), F32), V((RANK, DN_C), F32),
            V((NX, NY, 32, 128), F32), V((NX, NY, 24, 128), F32), V((NY, NX, 16, 128), F32), V((NY, NX, 16, 128), F32),
            V((NX, NY, 32, 128), F32), V((NX, NY, 24, 128), F32), V((NY, NX, 16, 128), F32),
            V((NX - 1, NY, 32, 128), F32), V((NX - 1, NY, 24, 128), F32), V((NY - 1, NX, 16, 128), F32),
            V((NY - 1, 32, 128), F32), V((NY, 24, 128), F32), V((NX, 16, 128), F32), V((NX - 1, 16, 128), F32),
            V((16, 128), F32), V((16, 128), F32), V((8, 128), F32), V((128, 128), F32),
            V((64, 128), F32), V((32, 128), F32), V((32, 128), F32), V((3, 8, 128), F32),
            V((NZ, 8, 128), F32), V((NY, 8, 128), F32), V((32, 128), F32),
            dma((9,)), *[dma((n,)) for n in (4, 4, 8, 8, 3, 3, 7, 7, 7, 7, 3, 3, 8, 8, 4, 4)],
            *[dma((n,)) for n in (3, 3, 7, 7, 7, 7, 3, 3)],
            *[dma((n,)) for n in (7, 7, 8, 8, 3, 3, 4, 4, 4, 4, 3, 3, 7, 7, 8, 8)], dma((2,)),
            *[dma] * 6,
        ],
        compiler_params=pltpu.CompilerParams(
            collective_id=0, has_side_effects=True, vmem_limit_bytes=32 * 1024 * 1024),
        name="exchange",
    )(*[pltpu.with_memory_space_constraint(a, pltpu.HBM) for a in (ug, ue, up_warm.T, dg, de, down_warm.T)])
    ua, ur, da, dr = pl.pallas_call(
        finish,
        out_shape=(
            jax.ShapeDtypeStruct((UP_R, UP_C), BF16),
            jax.ShapeDtypeStruct((UP_R, UP_C), F32),
            jax.ShapeDtypeStruct((DN_R, DN_C), BF16),
            jax.ShapeDtypeStruct((DN_R, DN_C), F32),
        ),
        in_specs=[vm] * 9,
        out_specs=(anywhere,) * 4,
        scratch_shapes=[
            V((UP_R, UP_C), BF16), V((UP_R, UP_C), F32), V((DN_R, DN_C), BF16), V((DN_R, DN_C), F32), dma((20,)),
        ],
        compiler_params=pltpu.CompilerParams(vmem_limit_bytes=32 * 1024 * 1024),
        name="finish",
    )(fa0, fa1, fb, wu, wd, ug, ue, dg, de)
    return ua, ur[None], da, dr[None]


def solution(mesh):
    return jax.shard_map(
        body,
        mesh=mesh,
        in_specs=(
            P("dp", None, "mp"),
            P("dp", None, "mp"),
            P("mp", None),
            P("dp", None, "mp"),
            P("dp", None, "mp"),
            P("mp", None),
        ),
        out_specs=(P(None, "mp"), P("dp", None, "mp"), P(None, "mp"), P("dp", None, "mp")),
        check_vma=False,
    )
```

```python
import jax
import jax.numpy as jnp
from jax import lax
from jax.experimental import pallas as pl
from jax.experimental.pallas import tpu as pltpu
from jax.sharding import PartitionSpec as P

F32 = jnp.float32
BF16 = jnp.bfloat16
HI = lax.Precision.HIGHEST
MESH = pl.DeviceIdType.MESH
NY, NX, NC, NZ = 8, 4, 2, 8
RANK = 32
UP_R, UP_C = 64, 3584
DN_R, DN_C = 128, 1024
HALF = UP_C // 2


def nt(a, b, precision=None):
    return lax.dot_general(a, b, (((1,), (1,)), ((), ())), preferred_element_type=F32, precision=precision)


def split(a):
    hi = a.astype(BF16)
    return hi, (a - hi.astype(F32)).astype(BF16)


def nt3(a, b):
    ah, al = split(a)
    bh, bl = split(b)
    return nt(ah, bh) + nt(ah, bl) + nt(al, bh)


def nt_acc(acc, wide, a, b):
    bh, bl = split(b)
    both = nt(wide, bh)
    return acc + both[:RANK] + both[RANK:] + nt(a, bl)


def eliminate(arrays, where, off):
    shape = (RANK, 128)
    row = lax.broadcasted_iota(jnp.int32, shape, 0)
    scale = jnp.ones(shape, F32)
    for first in range(0, RANK, 8):
        cols = [jnp.broadcast_to(arrays[where][:, off + first + m:off + first + m + 1], shape) for m in range(8)]
        for m in range(8):
            k = first + m
            pivot = cols[m][k:k + 1, :]
            factor = jnp.where(row > k, cols[m] * (1.0 / pivot), 0.0)
            for n in range(m + 1, 8):
                cols[n] = cols[n] - factor * cols[n][k:k + 1, :]
            arrays = [a - factor * a[k:k + 1, :] for a in arrays]
            scale = jnp.where(row == k, lax.rsqrt(pivot), scale)
    return arrays[0] * scale


def exchange(ug, ue, uw, dg, de, dw, FA0, FA1, FB, wu_out, wd_out, mu_out, md_out,
             MU, MD,
             vug, vue, vuw, vdg, vde, vdw, TU0, TU1, TD0, TD1, CU0, CU1, CD, XU0, XU1, YD, YU0, YU1, XD0, XD1,
             SA0, SA1, SB, SW, pt, pxr, pz, py, pg,
             in_sem, s_cu, r_cu, s_cd, r_cd, s_xu, r_xu, s_yd, r_yd, s_yu, r_yu, s_xd, r_xd, s_vu, r_vu, s_vd, r_vd,
             s_px, r_px, s_pz, r_pz, s_py, r_py, s_pa, r_pa,
             s_ay, r_ay, s_a1, r_a1, s_ax, r_ax, s_ac, r_ac, s_ad, r_ad, s_bx, r_bx, s_by, r_by, s_bc, r_bc, own_sem,
             s_wu, r_wu, s_wd, r_wd):
    d = lax.axis_index("dp")
    z = lax.axis_index("mp")
    c = lax.rem(d, 2)
    x = lax.rem(lax.div(d, 2), NX)
    y = lax.div(d, 8)
    other = 1 - c
    far_y = (4, 3, 5, 2, 6, 1, 7)
    far_x = (2, 1, 3)

    def at(yy, xx, cc):
        return ((yy * NX + xx) * NC + cc, z)

    partner = at(y, x, other)

    xs = [lax.rem(x + o, NX) for o in range(NX)]
    ys = [lax.rem(y + o, NY) for o in range(NY)]
    zs = [lax.rem(z + o, NZ) for o in range(NZ)]

    def xof(o):
        return xs[o % NX]

    def yof(o):
        return ys[o % NY]

    def xpeer(o):
        return at(y, xof(o), c)

    def ypeer(o):
        return at(yof(o), x, c)

    def zpeer(o):
        return (d, zs[o])

    pairs = []
    for half in range(2):
        cols = pl.ds(half * HALF, HALF)
        pairs += [(ug.at[:, cols], vug.at[:, cols]), (ue.at[:, cols], vue.at[:, cols]), (uw.at[:, cols], vuw.at[:, cols])]
    pairs += [(dg, vdg), (de, vde), (dw, vdw)]
    loads = [pltpu.make_async_copy(a, b, in_sem.at[i]) for i, (a, b) in enumerate(pairs)]
    bar = pltpu.get_barrier_semaphore()

    def greet(dev):
        pl.semaphore_signal(bar, 1, device_id=dev, device_id_type=MESH)

    for o in far_y[:3]:
        greet(zpeer(o))
        greet(ypeer(o))
    for cp in loads:
        cp.start()
    for o in far_y[3:]:
        greet(zpeer(o))
        greet(ypeer(o))
    for o in far_x:
        greet(at(y, xs[o], other))
        greet(xpeer(o))
    greet(partner)

    def down_part(b):
        cols = pl.ds(256 * b, 256)
        return vdg[:, cols].astype(F32) + vde[:, cols]

    def up_part(half, b):
        cols = pl.ds(half * HALF + 256 * b, 256)
        return vug[:, cols].astype(F32) + vue[:, cols]

    acc = jnp.zeros((RANK, UP_R), F32)
    for half in range(2):
        for cp in loads[3 * half:3 * half + 3]:
            cp.wait()
        for b in range(HALF // 256):
            hi, lo = split(vuw[:, pl.ds(half * HALF + 256 * b, 256)])
            acc = nt_acc(acc, jnp.concatenate([hi, lo], axis=0), hi, up_part(half, b))
    pt[0:32, :] = jnp.concatenate([acc, jnp.zeros((RANK, 64), F32)], axis=1)
    for cp in loads[6:]:
        cp.wait()
    acc = jnp.zeros((RANK, DN_R), F32)
    for b in range(DN_C // 256):
        hi, lo = split(vdw[:, pl.ds(256 * b, 256)])
        acc = nt_acc(acc, jnp.concatenate([hi, lo], axis=0), hi, down_part(b))
    pt[32:64, :] = acc

    pl.semaphore_wait(bar, 7 + 7 + 7)

    def describe(src, dst, ssem, rsem, dev):
        return pltpu.make_async_remote_copy(src_ref=src, dst_ref=dst, send_sem=ssem, recv_sem=rsem,
                                            device_id=dev, device_id_type=MESH)

    def remote(log, src, dst, ssem, rsem, dev):
        cp = describe(src, dst, ssem, rsem, dev)
        cp.start()
        log.append(cp)
        return cp

    sent = []
    cp_px = []
    for o, cc, k in ((2, other, 5), (2, c, 1), (1, other, 4), (3, other, 6), (1, c, 0), (3, c, 2), (0, other, 3)):
        rows = pl.ds(pl.multiple_of(cc * 32 + xs[o] * 8, 8), 8)
        cp_px.append(remote(sent, pt.at[rows], pxr.at[k], s_px.at[k], r_px.at[k], at(y, xs[o], cc)))

    for b in range(HALF // 256):
        parts = [up_part(0, b), up_part(1, b)]
        for half in range(2):
            MU[:, half * HALF + 256 * b:half * HALF + 256 * b + 256] = parts[half]
        stacked = jnp.concatenate(parts, axis=0)
        for s in range(2):
            turned = stacked[:, 128 * s:128 * (s + 1)].T
            for i in range(16):
                tile = (2 * b + s) * 16 + i
                q, u = tile // 7, tile % 7
                dst, r0 = (TU0, 8 * u) if u < 4 else (TU1, 8 * u - 32)
                dst[q // NY, q % NY, r0:r0 + 8, :] = turned[8 * i:8 * i + 8, :]

    for b in range(DN_C // 256):
        m = down_part(b)
        MD[:, 256 * b:256 * b + 256] = m
        for s in range(2):
            turned = m[:, 128 * s:128 * (s + 1)].T
            for i in range(4):
                q = (2 * b + s) * 4 + i
                TD0[q // NX, q % NX] = turned[32 * i:32 * i + 16, :]
                TD1[q // NX, q % NX] = turned[32 * i + 16:32 * i + 32, :]

    keep = [pltpu.make_async_copy(MU, mu_out, own_sem.at[2]), pltpu.make_async_copy(MD, md_out, own_sem.at[3])]
    for cp in keep:
        cp.start()
    mine = pl.ds(pl.multiple_of(x * 8, 8), 8)

    def proj_z(log):
        for cp in cp_px:
            cp.wait_recv()
        own = pt[pl.ds(pl.multiple_of(c * 32 + x * 8, 8), 8), :]
        pz[z] = ((own + pxr[0]) + (pxr[1] + pxr[2])) + ((pxr[3] + pxr[4]) + (pxr[5] + pxr[6]))
        return [remote(log, pz.at[z], pz.at[z], s_pz.at[o - 1], r_pz.at[o - 1], zpeer(o)) for o in far_y]

    def proj_y(log, cps):
        for cp in cps:
            cp.wait_recv()
        py[y] = ((pz[0] + pz[1]) + (pz[2] + pz[3])) + ((pz[4] + pz[5]) + (pz[6] + pz[7]))
        return [remote(log, py.at[y], py.at[y], s_py.at[o - 1], r_py.at[o - 1], ypeer(o)) for o in far_y]

    def proj_x(log, cps):
        for cp in cps:
            cp.wait_recv()
        pg[mine, :] = ((py[0] + py[1]) + (py[2] + py[3])) + ((py[4] + py[5]) + (py[6] + py[7]))
        return [remote(log, pg.at[mine], pg.at[mine], s_pa.at[o - 1], r_pa.at[o - 1], xpeer(o)) for o in far_x]

    lane = lax.broadcasted_iota(jnp.int32, (RANK, 128), 1)
    lane16 = lane[0:16]
    lane8 = lane[0:8]

    def local(log, src, dst, sem):
        cp = pltpu.make_async_copy(src, dst, sem)
        cp.start()
        log.append(cp)
        return cp

    def sum_merged(core, log):
        tu, tu_other = (TU0, TU1) if core == 0 else (TU1, TU0)
        td, td_other = (TD0, TD1) if core == 0 else (TD1, TD0)
        cu, cu_other = (CU0, CU1) if core == 0 else (CU1, CU0)
        xu = XU0 if core == 0 else XU1
        order = [(0, 2), (1, 4), (1, 3), (1, 5), (0, 1), (1, 2), (1, 6), (0, 3), (1, 1), (1, 7), (0, 0), (1, 0)]
        for kind, o in order:
            if kind == 0:
                remote(log, tu_other.at[xs[o]], cu_other.at[xs[o]], s_cu.at[o], r_cu.at[o], partner)
            else:
                remote(log, td_other.at[ys[o]], CD.at[ys[o]], s_cd.at[o], r_cd.at[o], partner)
        cp_xu, cp_yd = [], []
        for kind, o in order:
            if kind == 0:
                xx = xs[o]
                describe(tu.at[xx], cu.at[xx], s_cu.at[o], r_cu.at[o], partner).wait_recv()
                tu[xx] = tu[xx] + cu[xx]
                if o:
                    cp_xu.append(remote(log, tu.at[xx], xu.at[o - 1], s_xu.at[o - 1], r_xu.at[o - 1], xpeer(o)))
            else:
                yy = ys[o]
                describe(td.at[yy], CD.at[yy], s_cd.at[o], r_cd.at[o], partner).wait_recv()
                td[yy] = td[yy] + CD[yy]
                if o:
                    cp_yd.append(remote(log, td.at[yy], YD.at[o - 1], s_yd.at[o - 1], r_yd.at[o - 1], ypeer(o)))

        cp_py = proj_y(log, proj_z(log))

        for cp in cp_xu:
            cp.wait_recv()
        for o in far_y + (0,):
            yy = ys[o]
            tu[x, yy] = (tu[x, yy] + xu[0, yy]) + (xu[1, yy] + xu[2, yy])
            if core == 1:
                remote(log, tu.at[x, yy], YU1.at[o], s_vu.at[o], r_vu.at[o], at(yy, x, 0))
            elif o:
                remote(log, tu.at[x, yy], YU0.at[o - 1], s_yu.at[o - 1], r_yu.at[o - 1], at(yy, x, 0))

        cp_pa = proj_x(log, cp_py)

        for cp in cp_yd:
            cp.wait_recv()
        for o in far_x + (0,):
            xx = xs[o]
            tot = td[y, xx]
            for i in range(NY - 1):
                tot = tot + YD[i, xx]
            td[y, xx] = tot
            if core == 0:
                remote(log, td.at[y, xx], XD0.at[o], s_vd.at[o], r_vd.at[o], at(y, xx, 1))
            elif o:
                remote(log, td.at[y, xx], XD1.at[o - 1], s_xd.at[o - 1], r_xd.at[o - 1], at(y, xx, 1))
        for cp in cp_pa:
            cp.wait_recv()

    def pass_on(log, ref, k):
        return [remote(log, ref.at[x, ys[k]], ref.at[x, ys[k]], s_ax.at[8 * (o - 1) + k], r_ax.at[8 * (o - 1) + k],
                       xpeer(o)) for o in far_x]

    def gathered(cps):
        for cp in cps:
            cp.wait_recv()

    near_y = (1, 7, 2, 6, 3, 5, 4)

    @pl.when(c == 0)
    def _():
        log, near = [], []
        sum_merged(0, log)
        a = pg[...]
        gram = nt(a, a, HI)
        a = eliminate([jnp.concatenate([a[:, :64], gram, jnp.zeros((RANK, 32), F32)], axis=1)], 0, 64)
        left = jnp.where(lane < 64, a, 0.0)
        right = pltpu.roll(left, 64, axis=1)
        w = jnp.concatenate([left, right, left, right], axis=0)
        for o in far_y:
            describe(TU0.at[x, y], YU0.at[o - 1], s_yu.at[o - 1], r_yu.at[o - 1], partner).wait_recv()
        for o in far_y + (0,):
            describe(TU1.at[x, y], YU1.at[o], s_vu.at[o], r_vu.at[o], partner).wait_recv()
        low = TU0[x, y]
        for i in range(NY - 1):
            low = low + YU0[i]
        high = YU1[0]
        for i in range(1, NY):
            high = high + YU1[i]
        r = nt(jnp.concatenate([low, high], axis=0) * (1.0 / 64.0), w, HI)
        SA1[...] = jnp.where(lane16 < 64, r[16:32], jnp.concatenate([r[48:56], jnp.zeros((8, 128), F32)], axis=0))
        SA0[...] = jnp.where(lane16 < 64, r[0:16], r[32:48])

        before = len(log)
        cp_ay = {}
        for o in far_y:
            cp_ay[o] = remote(log, SA0, FA0.at[x, y], s_ay.at[o - 1], r_ay.at[o - 1], ypeer(o))
            remote(log, SA1, FA1.at[x, y], s_a1.at[o], r_a1.at[o], at(ys[o], x, 1))
        remote(log, SA1, FA1.at[x, y], s_a1.at[0], r_a1.at[0], partner)
        local(near, SA0, FA0.at[x, y], own_sem.at[0])
        near[0].wait()
        pieces = [pass_on(log, FA0, 0)]
        for k in near_y:
            cp_ay[NY - k].wait_recv()
            pieces.append(pass_on(log, FA0, k))
        remote(log, FA0.at[x], FA0.at[x], s_ac.at[0], r_ac.at[0], partner)
        SW[...] = w.T
        remote(log, SW, wu_out, s_wu, r_wu, partner)
        local(near, SW, wu_out, own_sem.at[1])
        for cp in sent + log[:before]:
            cp.wait_send()
        for cp in keep:
            cp.wait()
        for i, o in ((1, 1), (2, 3), (0, 2)):
            gathered([p[i] for p in pieces])
            xx = xof(NX - o)
            remote(log, FA0.at[xx], FA0.at[xx], s_ac.at[o], r_ac.at[o], partner)
        describe(SW, wd_out, s_wd, r_wd, partner).wait_recv()
        for o in range(NY):
            describe(FB.at[ys[o]], FB.at[ys[o]], s_bc.at[o], r_bc.at[o], partner).wait_recv()
        for o in range(NX):
            describe(FA1.at[xs[o]], FA1.at[xs[o]], s_ad.at[o], r_ad.at[o], partner).wait_recv()
        for cp in log[before:]:
            cp.wait_send()
        near[1].wait()

    @pl.when(c == 1)
    def _():
        log, near = [], []
        sum_merged(1, log)
        a = pg[...]
        gram = nt(a, a, HI)
        a = eliminate([a, jnp.concatenate([gram, jnp.zeros((RANK, 96), F32)], axis=1)], 1, 0)
        w = jnp.concatenate([a, a, a, a], axis=0)
        for o in far_x:
            describe(TD1.at[y, x], XD1.at[o - 1], s_xd.at[o - 1], r_xd.at[o - 1], partner).wait_recv()
        for o in far_x + (0,):
            describe(TD0.at[y, x], XD0.at[o], s_vd.at[o], r_vd.at[o], partner).wait_recv()
        low = (XD0[0] + XD0[1]) + (XD0[2] + XD0[3])
        high = (TD1[y, x] + XD1[0]) + (XD1[1] + XD1[2])
        r = nt(jnp.concatenate([low, high], axis=0) * (1.0 / 64.0), w, HI)
        low = jnp.where(lane8 < 32, r[0:8], r[8:16])
        high = jnp.where(lane8 < 96, r[16:24], r[24:32])
        SB[...] = jnp.where(lane8 < 64, low, high)

        before = len(log)
        cp_bx = [remote(log, SB, FB.at[y, x], s_bx.at[o - 1], r_bx.at[o - 1], xpeer(o)) for o in far_x]
        local(near, SB, FB.at[y, x], own_sem.at[0])
        SW[...] = w.T
        remote(log, SW, wd_out, s_wd, r_wd, partner)
        local(near, SW, wd_out, own_sem.at[1])
        near[0].wait()
        for cp in cp_bx:
            cp.wait_recv()
        cp_by = [remote(log, FB.at[y], FB.at[y], s_by.at[o - 1], r_by.at[o - 1], ypeer(o)) for o in far_y]
        pieces = []
        for k in (0,) + near_y:
            o = (NY - k) % NY
            describe(SA1, FA1.at[x, ys[k]], s_a1.at[o], r_a1.at[o], partner).wait_recv()
            pieces.append(pass_on(log, FA1, k))
        remote(log, FA1.at[x], FA1.at[x], s_ad.at[0], r_ad.at[0], partner)
        remote(log, FB.at[y], FB.at[y], s_bc.at[0], r_bc.at[0], partner)
        for cp in sent + log[:before]:
            cp.wait_send()
        for cp in keep:
            cp.wait()
        for cp, o in zip(cp_by, far_y):
            cp.wait_recv()
            yy = yof(NY - o)
            remote(log, FB.at[yy], FB.at[yy], s_bc.at[o], r_bc.at[o], partner)
        for i, o in ((1, 1), (2, 3), (0, 2)):
            gathered([p[i] for p in pieces])
            xx = xof(NX - o)
            remote(log, FA1.at[xx], FA1.at[xx], s_ad.at[o], r_ad.at[o], partner)
        describe(SW, wu_out, s_wu, r_wu, partner).wait_recv()
        for o in range(NX):
            describe(FA0.at[xs[o]], FA0.at[xs[o]], s_ac.at[o], r_ac.at[o], partner).wait_recv()
        for cp in log[before:]:
            cp.wait_send()
        near[1].wait()


def finish(fa0, fa1, fb, wu, wd, mu, md, ua, ur, da, dr, bua, bur, bda, bdr, sem):
    lane = lax.broadcasted_iota(jnp.int32, (8, 128), 1)
    started = []

    def store(src, dst, cols):
        cp = pltpu.make_async_copy(src.at[:, cols], dst.at[:, cols], sem.at[len(started)])
        cp.start()
        started.append(cp)

    def up_tile(tile):
        q, u = tile // 7, tile % 7
        src, r0 = (fa0, fa1)[u % 4 // 2], (u % 2) * 8
        return jnp.where(lane // 64 == u // 4, src[q // NY, q % NY, r0:r0 + 8, :], 0.0)

    def down_tile(tile):
        q, u = tile // 4, tile % 4
        return jnp.where(lane // 32 == u, fb[q // NX, q % NX], 0.0)

    for first, last in ((0, 2), (2, 4), (4, 6), (6, 7)):
        for b in range(first, last):
            delta = nt3(wu[...], jnp.concatenate([up_tile(32 * b + i) for i in range(32)], axis=0))
            for half in range(2):
                cols = pl.ds(half * HALF + 256 * b, 256)
                part = delta[64 * half:64 * half + 64, :]
                bua[:, cols] = part.astype(BF16)
                bur[:, cols] = mu[:, cols] - part
        for half in range(2):
            cols = pl.ds(half * HALF + 256 * first, 256 * (last - first))
            store(bua, ua, cols)
            store(bur, ur, cols)
    for first, last in ((0, 2), (2, 4)):
        for b in range(first, last):
            cols = pl.ds(256 * b, 256)
            delta = nt3(wd[...], jnp.concatenate([down_tile(32 * b + i) for i in range(32)], axis=0))
            bda[:, cols] = delta.astype(BF16)
            bdr[:, cols] = md[:, cols] - delta
        cols = pl.ds(256 * first, 256 * (last - first))
        store(bda, da, cols)
        store(bdr, dr, cols)
    for cp in started:
        cp.wait()


def body(up_grad, up_error, up_warm, down_grad, down_error, down_warm):
    ug, ue, dg, de = up_grad[0], up_error[0], down_grad[0], down_error[0]
    vm = pl.BlockSpec(memory_space=pltpu.VMEM)
    hbm = pl.BlockSpec(memory_space=pltpu.HBM)
    anywhere = pl.BlockSpec(memory_space=pl.ANY)
    dma = pltpu.SemaphoreType.DMA
    V = pltpu.VMEM
    fa0, fa1, fb, wu, wd, mu, md = pl.pallas_call(
        exchange,
        out_shape=(
            jax.ShapeDtypeStruct((NX, NY, 16, 128), F32),
            jax.ShapeDtypeStruct((NX, NY, 16, 128), F32),
            jax.ShapeDtypeStruct((NY, NX, 8, 128), F32),
            jax.ShapeDtypeStruct((128, 128), F32),
            jax.ShapeDtypeStruct((128, 128), F32),
            jax.ShapeDtypeStruct((UP_R, UP_C), F32),
            jax.ShapeDtypeStruct((DN_R, DN_C), F32),
        ),
        in_specs=[hbm] * 6,
        out_specs=(anywhere,) * 7,
        scratch_shapes=[
            V((UP_R, UP_C), F32), V((DN_R, DN_C), F32),
            V((UP_R, UP_C), BF16), V((UP_R, UP_C), F32), V((RANK, UP_C), F32),
            V((DN_R, DN_C), BF16), V((DN_R, DN_C), F32), V((RANK, DN_C), F32),
            V((NX, NY, 32, 128), F32), V((NX, NY, 24, 128), F32), V((NY, NX, 16, 128), F32), V((NY, NX, 16, 128), F32),
            V((NX, NY, 32, 128), F32), V((NX, NY, 24, 128), F32), V((NY, NX, 16, 128), F32),
            V((NX - 1, NY, 32, 128), F32), V((NX - 1, NY, 24, 128), F32), V((NY - 1, NX, 16, 128), F32),
            V((NY - 1, 32, 128), F32), V((NY, 24, 128), F32), V((NX, 16, 128), F32), V((NX - 1, 16, 128), F32),
            V((16, 128), F32), V((16, 128), F32), V((8, 128), F32), V((128, 128), F32),
            V((64, 128), F32), V((7, 8, 128), F32),
            V((NZ, 8, 128), F32), V((NY, 8, 128), F32), V((32, 128), F32),
            dma((9,)), *[dma((n,)) for n in (4, 4, 8, 8, 3, 3, 7, 7, 7, 7, 3, 3, 8, 8, 4, 4)],
            *[dma((n,)) for n in (7, 7, 7, 7, 7, 7, 3, 3)],
            *[dma((n,)) for n in (7, 7, 8, 8, 24, 24, 4, 4, 4, 4, 3, 3, 7, 7, 8, 8)], dma((4,)),
            *[dma] * 4,
        ],
        compiler_params=pltpu.CompilerParams(
            collective_id=0, has_side_effects=True, vmem_limit_bytes=32 * 1024 * 1024),
        name="exchange",
    )(*[pltpu.with_memory_space_constraint(a, pltpu.HBM) for a in (ug, ue, up_warm.T, dg, de, down_warm.T)])
    ua, ur, da, dr = pl.pallas_call(
        finish,
        out_shape=(
            jax.ShapeDtypeStruct((UP_R, UP_C), BF16),
            jax.ShapeDtypeStruct((UP_R, UP_C), F32),
            jax.ShapeDtypeStruct((DN_R, DN_C), BF16),
            jax.ShapeDtypeStruct((DN_R, DN_C), F32),
        ),
        in_specs=[vm] * 7,
        out_specs=(anywhere,) * 4,
        scratch_shapes=[
            V((UP_R, UP_C), BF16), V((UP_R, UP_C), F32), V((DN_R, DN_C), BF16), V((DN_R, DN_C), F32), dma((20,)),
        ],
        compiler_params=pltpu.CompilerParams(vmem_limit_bytes=32 * 1024 * 1024),
        name="finish",
    )(fa0, fa1, fb, wu, wd, mu, md)
    return ua, ur[None], da, dr[None]


def solution(mesh):
    return jax.shard_map(
        body,
        mesh=mesh,
        in_specs=(
            P("dp", None, "mp"),
            P("dp", None, "mp"),
            P("mp", None),
            P("dp", None, "mp"),
            P("dp", None, "mp"),
            P("mp", None),
        ),
        out_specs=(P(None, "mp"), P("dp", None, "mp"), P(None, "mp"), P("dp", None, "mp")),
        check_vma=False,
    )
```

```python
import jax
import jax.numpy as jnp
from jax import lax
from jax.experimental import pallas as pl
from jax.experimental.pallas import tpu as pltpu
from jax.sharding import PartitionSpec as P

F32 = jnp.float32
BF16 = jnp.bfloat16
HI = lax.Precision.HIGHEST
MESH = pl.DeviceIdType.MESH
NY, NX, NC, NZ = 8, 4, 2, 8
RANK = 32
UP_R, UP_C = 64, 3584
DN_R, DN_C = 128, 1024
HALF = UP_C // 2


def nt(a, b, precision=None):
    return lax.dot_general(a, b, (((1,), (1,)), ((), ())), preferred_element_type=F32, precision=precision)


def split(a):
    hi = a.astype(BF16)
    return hi, (a - hi.astype(F32)).astype(BF16)


def nt3(a, b):
    ah, al = split(a)
    bh, bl = split(b)
    return nt(ah, bh) + nt(ah, bl) + nt(al, bh)


def nt_acc(acc, wide, a, b):
    bh, bl = split(b)
    both = nt(wide, bh)
    return acc + both[:RANK] + both[RANK:] + nt(a, bl)


def eliminate(arrays, where, off):
    shape = (RANK, 128)
    row = lax.broadcasted_iota(jnp.int32, shape, 0)
    scale = jnp.ones(shape, F32)
    for first in range(0, RANK, 8):
        cols = [jnp.broadcast_to(arrays[where][:, off + first + m:off + first + m + 1], shape) for m in range(8)]
        for m in range(8):
            k = first + m
            pivot = cols[m][k:k + 1, :]
            factor = jnp.where(row > k, cols[m] * (1.0 / pivot), 0.0)
            for n in range(m + 1, 8):
                cols[n] = cols[n] - factor * cols[n][k:k + 1, :]
            arrays = [a - factor * a[k:k + 1, :] for a in arrays]
            scale = jnp.where(row == k, lax.rsqrt(pivot), scale)
    return arrays[0] * scale


def exchange(ug, ue, uw, dg, de, dw, FA0, FA1, FB, wu_out, wd_out, mu_out, md_out,
             MU, MD,
             vug, vue, vuw, vdg, vde, vdw, TU0, TU1, TD0, TD1, CU0, CU1, CD, XU0, XU1, YD, YU0, YU1, XD0, XD1,
             SA0, SA1, SB, SW, pt, pxr, pz, py, pg,
             in_sem, s_cu, r_cu, s_cd, r_cd, s_xu, r_xu, s_yd, r_yd, s_yu, r_yu, s_xd, r_xd, s_vu, r_vu, s_vd, r_vd,
             s_px, r_px, s_pz, r_pz, s_py, r_py, s_pa, r_pa,
             s_ay, r_ay, s_a1, r_a1, s_ax, r_ax, s_ac, r_ac, s_ad, r_ad, s_bx, r_bx, s_by, r_by, s_bc, r_bc, own_sem,
             s_wu, r_wu, s_wd, r_wd):
    d = lax.axis_index("dp")
    z = lax.axis_index("mp")
    c = lax.rem(d, 2)
    x = lax.rem(lax.div(d, 2), NX)
    y = lax.div(d, 8)
    other = 1 - c
    far_y = (4, 3, 5, 2, 6, 1, 7)
    far_x = (2, 1, 3)

    def at(yy, xx, cc):
        return ((yy * NX + xx) * NC + cc, z)

    partner = at(y, x, other)

    xs = [lax.rem(x + o, NX) for o in range(NX)]
    ys = [lax.rem(y + o, NY) for o in range(NY)]
    zs = [lax.rem(z + o, NZ) for o in range(NZ)]

    def xof(o):
        return xs[o % NX]

    def yof(o):
        return ys[o % NY]

    def xpeer(o):
        return at(y, xof(o), c)

    def ypeer(o):
        return at(yof(o), x, c)

    def zpeer(o):
        return (d, zs[o])

    pairs = []
    for half in range(2):
        cols = pl.ds(half * HALF, HALF)
        pairs += [(ug.at[:, cols], vug.at[:, cols]), (ue.at[:, cols], vue.at[:, cols]), (uw.at[:, cols], vuw.at[:, cols])]
    pairs += [(dg, vdg), (de, vde), (dw, vdw)]
    loads = [pltpu.make_async_copy(a, b, in_sem.at[i]) for i, (a, b) in enumerate(pairs)]
    bar = pltpu.get_barrier_semaphore()

    def greet(dev):
        pl.semaphore_signal(bar, 1, device_id=dev, device_id_type=MESH)

    for o in far_y[:3]:
        greet(zpeer(o))
        greet(ypeer(o))
    for cp in loads:
        cp.start()
    for o in far_y[3:]:
        greet(zpeer(o))
        greet(ypeer(o))
    for o in far_x:
        greet(at(y, xs[o], other))
        greet(xpeer(o))
    greet(partner)

    def down_part(b):
        cols = pl.ds(256 * b, 256)
        return vdg[:, cols].astype(F32) + vde[:, cols]

    def up_part(half, b):
        cols = pl.ds(half * HALF + 256 * b, 256)
        return vug[:, cols].astype(F32) + vue[:, cols]

    acc = jnp.zeros((RANK, UP_R), F32)
    for half in range(2):
        for cp in loads[3 * half:3 * half + 3]:
            cp.wait()
        for b in range(HALF // 256):
            hi, lo = split(vuw[:, pl.ds(half * HALF + 256 * b, 256)])
            acc = nt_acc(acc, jnp.concatenate([hi, lo], axis=0), hi, up_part(half, b))
    pt[0:32, :] = jnp.concatenate([acc, jnp.zeros((RANK, 64), F32)], axis=1)
    for cp in loads[6:]:
        cp.wait()
    acc = jnp.zeros((RANK, DN_R), F32)
    for b in range(DN_C // 256):
        hi, lo = split(vdw[:, pl.ds(256 * b, 256)])
        acc = nt_acc(acc, jnp.concatenate([hi, lo], axis=0), hi, down_part(b))
    pt[32:64, :] = acc

    pl.semaphore_wait(bar, 7 + 7 + 7)

    def describe(src, dst, ssem, rsem, dev):
        return pltpu.make_async_remote_copy(src_ref=src, dst_ref=dst, send_sem=ssem, recv_sem=rsem,
                                            device_id=dev, device_id_type=MESH)

    def remote(log, src, dst, ssem, rsem, dev):
        cp = describe(src, dst, ssem, rsem, dev)
        cp.start()
        log.append(cp)
        return cp

    sent = []
    cp_px = []
    for o, cc, k in ((2, other, 5), (2, c, 1), (1, other, 4), (3, other, 6), (1, c, 0), (3, c, 2), (0, other, 3)):
        rows = pl.ds(pl.multiple_of(cc * 32 + xs[o] * 8, 8), 8)
        cp_px.append(remote(sent, pt.at[rows], pxr.at[k], s_px.at[k], r_px.at[k], at(y, xs[o], cc)))

    for b in range(HALF // 256):
        parts = [up_part(0, b), up_part(1, b)]
        for half in range(2):
            MU[:, half * HALF + 256 * b:half * HALF + 256 * b + 256] = parts[half]
        stacked = jnp.concatenate(parts, axis=0)
        for s in range(2):
            turned = stacked[:, 128 * s:128 * (s + 1)].T
            for i in range(16):
                tile = (2 * b + s) * 16 + i
                q, u = tile // 7, tile % 7
                dst, r0 = (TU0, 8 * u) if u < 4 else (TU1, 8 * u - 32)
                dst[q // NY, q % NY, r0:r0 + 8, :] = turned[8 * i:8 * i + 8, :]

    for b in range(DN_C // 256):
        m = down_part(b)
        MD[:, 256 * b:256 * b + 256] = m
        for s in range(2):
            turned = m[:, 128 * s:128 * (s + 1)].T
            for i in range(4):
                q = (2 * b + s) * 4 + i
                TD0[q // NX, q % NX] = turned[32 * i:32 * i + 16, :]
                TD1[q // NX, q % NX] = turned[32 * i + 16:32 * i + 32, :]

    keep = [pltpu.make_async_copy(MU, mu_out, own_sem.at[2]), pltpu.make_async_copy(MD, md_out, own_sem.at[3])]
    for cp in keep:
        cp.start()
    mine = pl.ds(pl.multiple_of(x * 8, 8), 8)

    def proj_z(log):
        for cp in cp_px:
            cp.wait_recv()
        own = pt[pl.ds(pl.multiple_of(c * 32 + x * 8, 8), 8), :]
        pz[z] = ((own + pxr[0]) + (pxr[1] + pxr[2])) + ((pxr[3] + pxr[4]) + (pxr[5] + pxr[6]))
        return [remote(log, pz.at[z], pz.at[z], s_pz.at[o - 1], r_pz.at[o - 1], zpeer(o)) for o in far_y]

    def proj_y(log, cps):
        for cp in cps:
            cp.wait_recv()
        py[y] = ((pz[0] + pz[1]) + (pz[2] + pz[3])) + ((pz[4] + pz[5]) + (pz[6] + pz[7]))
        return [remote(log, py.at[y], py.at[y], s_py.at[o - 1], r_py.at[o - 1], ypeer(o)) for o in far_y]

    def proj_x(log, cps):
        for cp in cps:
            cp.wait_recv()
        pg[mine, :] = ((py[0] + py[1]) + (py[2] + py[3])) + ((py[4] + py[5]) + (py[6] + py[7]))
        return [remote(log, pg.at[mine], pg.at[mine], s_pa.at[o - 1], r_pa.at[o - 1], xpeer(o)) for o in far_x]

    lane = lax.broadcasted_iota(jnp.int32, (RANK, 128), 1)
    lane16 = lane[0:16]
    lane8 = lane[0:8]

    def local(log, src, dst, sem):
        cp = pltpu.make_async_copy(src, dst, sem)
        cp.start()
        log.append(cp)
        return cp

    def sum_merged(core, log):
        tu, tu_other = (TU0, TU1) if core == 0 else (TU1, TU0)
        td, td_other = (TD0, TD1) if core == 0 else (TD1, TD0)
        cu, cu_other = (CU0, CU1) if core == 0 else (CU1, CU0)
        xu = XU0 if core == 0 else XU1
        order = [(0, 2), (1, 4), (1, 3), (1, 5), (0, 1), (1, 2), (1, 6), (0, 3), (1, 1), (1, 7), (0, 0), (1, 0)]
        for kind, o in order:
            if kind == 0:
                remote(log, tu_other.at[xs[o]], cu_other.at[xs[o]], s_cu.at[o], r_cu.at[o], partner)
            else:
                remote(log, td_other.at[ys[o]], CD.at[ys[o]], s_cd.at[o], r_cd.at[o], partner)
        cp_xu, cp_yd = [], []
        for kind, o in order:
            if kind == 0:
                xx = xs[o]
                describe(tu.at[xx], cu.at[xx], s_cu.at[o], r_cu.at[o], partner).wait_recv()
                tu[xx] = tu[xx] + cu[xx]
                if o:
                    cp_xu.append(remote(log, tu.at[xx], xu.at[o - 1], s_xu.at[o - 1], r_xu.at[o - 1], xpeer(o)))
            else:
                yy = ys[o]
                describe(td.at[yy], CD.at[yy], s_cd.at[o], r_cd.at[o], partner).wait_recv()
                td[yy] = td[yy] + CD[yy]
                if o:
                    cp_yd.append(remote(log, td.at[yy], YD.at[o - 1], s_yd.at[o - 1], r_yd.at[o - 1], ypeer(o)))

        cp_py = proj_y(log, proj_z(log))

        for cp in cp_xu:
            cp.wait_recv()
        for o in far_y + (0,):
            yy = ys[o]
            tu[x, yy] = (tu[x, yy] + xu[0, yy]) + (xu[1, yy] + xu[2, yy])
            if core == 1:
                remote(log, tu.at[x, yy], YU1.at[o], s_vu.at[o], r_vu.at[o], at(yy, x, 0))
            elif o:
                remote(log, tu.at[x, yy], YU0.at[o - 1], s_yu.at[o - 1], r_yu.at[o - 1], at(yy, x, 0))

        cp_pa = proj_x(log, cp_py)

        for cp in cp_yd:
            cp.wait_recv()
        for o in far_x + (0,):
            xx = xs[o]
            tot = td[y, xx]
            for i in range(NY - 1):
                tot = tot + YD[i, xx]
            td[y, xx] = tot
            if core == 0:
                remote(log, td.at[y, xx], XD0.at[o], s_vd.at[o], r_vd.at[o], at(y, xx, 1))
            elif o:
                remote(log, td.at[y, xx], XD1.at[o - 1], s_xd.at[o - 1], r_xd.at[o - 1], at(y, xx, 1))
        for cp in cp_pa:
            cp.wait_recv()

    def pass_on(log, ref, k):
        return [remote(log, ref.at[x, ys[k]], ref.at[x, ys[k]], s_ax.at[8 * (o - 1) + k], r_ax.at[8 * (o - 1) + k],
                       xpeer(o)) for o in far_x]

    def gathered(cps):
        for cp in cps:
            cp.wait_recv()

    near_y = (1, 7, 2, 6, 3, 5, 4)

    @pl.when(c == 0)
    def _():
        log, near = [], []
        sum_merged(0, log)
        a = pg[...]
        gram = nt(a, a, HI)
        a = eliminate([jnp.concatenate([a[:, :64], gram, jnp.zeros((RANK, 32), F32)], axis=1)], 0, 64)
        left = jnp.where(lane < 64, a, 0.0)
        right = pltpu.roll(left, 64, axis=1)
        w = jnp.concatenate([left, right, left, right], axis=0)
        for o in far_y:
            describe(TU0.at[x, y], YU0.at[o - 1], s_yu.at[o - 1], r_yu.at[o - 1], partner).wait_recv()
        for o in far_y + (0,):
            describe(TU1.at[x, y], YU1.at[o], s_vu.at[o], r_vu.at[o], partner).wait_recv()
        low = TU0[x, y]
        for i in range(NY - 1):
            low = low + YU0[i]
        high = YU1[0]
        for i in range(1, NY):
            high = high + YU1[i]
        r = nt(jnp.concatenate([low, high], axis=0) * (1.0 / 64.0), w, HI)
        SA1[...] = jnp.where(lane16 < 64, r[16:32], jnp.concatenate([r[48:56], jnp.zeros((8, 128), F32)], axis=0))
        SA0[...] = jnp.where(lane16 < 64, r[0:16], r[32:48])

        before = len(log)
        cp_ay = {}
        for o in far_y:
            cp_ay[o] = remote(log, SA0, FA0.at[x, y], s_ay.at[o - 1], r_ay.at[o - 1], ypeer(o))
            remote(log, SA1, FA1.at[x, y], s_a1.at[o], r_a1.at[o], at(ys[o], x, 1))
        remote(log, SA1, FA1.at[x, y], s_a1.at[0], r_a1.at[0], partner)
        local(near, SA0, FA0.at[x, y], own_sem.at[0])
        near[0].wait()
        pieces = [pass_on(log, FA0, 0)]
        for k in near_y:
            cp_ay[NY - k].wait_recv()
            pieces.append(pass_on(log, FA0, k))
        remote(log, FA0.at[x], FA0.at[x], s_ac.at[0], r_ac.at[0], partner)
        SW[...] = w.T
        remote(log, SW, wu_out, s_wu, r_wu, partner)
        local(near, SW, wu_out, own_sem.at[1])
        for cp in sent + log[:before]:
            cp.wait_send()
        for cp in keep:
            cp.wait()
        for i, o in ((1, 1), (2, 3), (0, 2)):
            gathered([p[i] for p in pieces])
            xx = xof(NX - o)
            remote(log, FA0.at[xx], FA0.at[xx], s_ac.at[o], r_ac.at[o], partner)
        describe(SW, wd_out, s_wd, r_wd, partner).wait_recv()
        for o in range(NY):
            describe(FB.at[ys[o]], FB.at[ys[o]], s_bc.at[o], r_bc.at[o], partner).wait_recv()
        for o in range(NX):
            describe(FA1.at[xs[o]], FA1.at[xs[o]], s_ad.at[o], r_ad.at[o], partner).wait_recv()
        for cp in log[before:]:
            cp.wait_send()
        near[1].wait()

    @pl.when(c == 1)
    def _():
        log, near = [], []
        sum_merged(1, log)
        a = pg[...]
        gram = nt(a, a, HI)
        a = eliminate([a, jnp.concatenate([gram, jnp.zeros((RANK, 96), F32)], axis=1)], 1, 0)
        w = jnp.concatenate([a, a, a, a], axis=0)
        for o in far_x:
            describe(TD1.at[y, x], XD1.at[o - 1], s_xd.at[o - 1], r_xd.at[o - 1], partner).wait_recv()
        for o in far_x + (0,):
            describe(TD0.at[y, x], XD0.at[o], s_vd.at[o], r_vd.at[o], partner).wait_recv()
        low = (XD0[0] + XD0[1]) + (XD0[2] + XD0[3])
        high = (TD1[y, x] + XD1[0]) + (XD1[1] + XD1[2])
        r = nt(jnp.concatenate([low, high], axis=0) * (1.0 / 64.0), w, HI)
        low = jnp.where(lane8 < 32, r[0:8], r[8:16])
        high = jnp.where(lane8 < 96, r[16:24], r[24:32])
        SB[...] = jnp.where(lane8 < 64, low, high)

        before = len(log)
        cp_bx = [remote(log, SB, FB.at[y, x], s_bx.at[o - 1], r_bx.at[o - 1], xpeer(o)) for o in far_x]
        local(near, SB, FB.at[y, x], own_sem.at[0])
        SW[...] = w.T
        remote(log, SW, wd_out, s_wd, r_wd, partner)
        local(near, SW, wd_out, own_sem.at[1])
        near[0].wait()
        pieces = []
        for k in (0,) + near_y:
            o = (NY - k) % NY
            describe(SA1, FA1.at[x, ys[k]], s_a1.at[o], r_a1.at[o], partner).wait_recv()
            pieces.append(pass_on(log, FA1, k))
            if k == 7:
                for cp in cp_bx:
                    cp.wait_recv()
                cp_by = [remote(log, FB.at[y], FB.at[y], s_by.at[p - 1], r_by.at[p - 1], ypeer(p)) for p in far_y]
        remote(log, FA1.at[x], FA1.at[x], s_ad.at[0], r_ad.at[0], partner)
        remote(log, FB.at[y], FB.at[y], s_bc.at[0], r_bc.at[0], partner)
        for cp in sent + log[:before]:
            cp.wait_send()
        for cp in keep:
            cp.wait()
        for cp, o in zip(cp_by, far_y):
            cp.wait_recv()
            yy = yof(NY - o)
            remote(log, FB.at[yy], FB.at[yy], s_bc.at[o], r_bc.at[o], partner)
        for i, o in ((1, 1), (2, 3), (0, 2)):
            gathered([p[i] for p in pieces])
            xx = xof(NX - o)
            remote(log, FA1.at[xx], FA1.at[xx], s_ad.at[o], r_ad.at[o], partner)
        describe(SW, wu_out, s_wu, r_wu, partner).wait_recv()
        for o in range(NX):
            describe(FA0.at[xs[o]], FA0.at[xs[o]], s_ac.at[o], r_ac.at[o], partner).wait_recv()
        for cp in log[before:]:
            cp.wait_send()
        near[1].wait()


def finish(fa0, fa1, fb, wu, wd, mu, md, ua, ur, da, dr, bua, bur, bda, bdr, sem):
    lane = lax.broadcasted_iota(jnp.int32, (8, 128), 1)
    started = []

    def store(src, dst, cols):
        cp = pltpu.make_async_copy(src.at[:, cols], dst.at[:, cols], sem.at[len(started)])
        cp.start()
        started.append(cp)

    def up_tile(tile):
        q, u = tile // 7, tile % 7
        src, r0 = (fa0, fa1)[u % 4 // 2], (u % 2) * 8
        return jnp.where(lane // 64 == u // 4, src[q // NY, q % NY, r0:r0 + 8, :], 0.0)

    def down_tile(tile):
        q, u = tile // 4, tile % 4
        return jnp.where(lane // 32 == u, fb[q // NX, q % NX], 0.0)

    for first, last in ((0, 2), (2, 4), (4, 6), (6, 7)):
        for b in range(first, last):
            delta = nt3(wu[...], jnp.concatenate([up_tile(32 * b + i) for i in range(32)], axis=0))
            for half in range(2):
                cols = pl.ds(half * HALF + 256 * b, 256)
                part = delta[64 * half:64 * half + 64, :]
                bua[:, cols] = part.astype(BF16)
                bur[:, cols] = mu[:, cols] - part
        for half in range(2):
            cols = pl.ds(half * HALF + 256 * first, 256 * (last - first))
            store(bua, ua, cols)
            store(bur, ur, cols)
    for first, last in ((0, 2), (2, 4)):
        for b in range(first, last):
            cols = pl.ds(256 * b, 256)
            delta = nt3(wd[...], jnp.concatenate([down_tile(32 * b + i) for i in range(32)], axis=0))
            bda[:, cols] = delta.astype(BF16)
            bdr[:, cols] = md[:, cols] - delta
        cols = pl.ds(256 * first, 256 * (last - first))
        store(bda, da, cols)
        store(bdr, dr, cols)
    for cp in started:
        cp.wait()


def body(up_grad, up_error, up_warm, down_grad, down_error, down_warm):
    ug, ue, dg, de = up_grad[0], up_error[0], down_grad[0], down_error[0]
    vm = pl.BlockSpec(memory_space=pltpu.VMEM)
    hbm = pl.BlockSpec(memory_space=pltpu.HBM)
    anywhere = pl.BlockSpec(memory_space=pl.ANY)
    dma = pltpu.SemaphoreType.DMA
    V = pltpu.VMEM
    fa0, fa1, fb, wu, wd, mu, md = pl.pallas_call(
        exchange,
        out_shape=(
            jax.ShapeDtypeStruct((NX, NY, 16, 128), F32),
            jax.ShapeDtypeStruct((NX, NY, 16, 128), F32),
            jax.ShapeDtypeStruct((NY, NX, 8, 128), F32),
            jax.ShapeDtypeStruct((128, 128), F32),
            jax.ShapeDtypeStruct((128, 128), F32),
            jax.ShapeDtypeStruct((UP_R, UP_C), F32),
            jax.ShapeDtypeStruct((DN_R, DN_C), F32),
        ),
        in_specs=[hbm] * 6,
        out_specs=(anywhere,) * 7,
        scratch_shapes=[
            V((UP_R, UP_C), F32), V((DN_R, DN_C), F32),
            V((UP_R, UP_C), BF16), V((UP_R, UP_C), F32), V((RANK, UP_C), F32),
            V((DN_R, DN_C), BF16), V((DN_R, DN_C), F32), V((RANK, DN_C), F32),
            V((NX, NY, 32, 128), F32), V((NX, NY, 24, 128), F32), V((NY, NX, 16, 128), F32), V((NY, NX, 16, 128), F32),
            V((NX, NY, 32, 128), F32), V((NX, NY, 24, 128), F32), V((NY, NX, 16, 128), F32),
            V((NX - 1, NY, 32, 128), F32), V((NX - 1, NY, 24, 128), F32), V((NY - 1, NX, 16, 128), F32),
            V((NY - 1, 32, 128), F32), V((NY, 24, 128), F32), V((NX, 16, 128), F32), V((NX - 1, 16, 128), F32),
            V((16, 128), F32), V((16, 128), F32), V((8, 128), F32), V((128, 128), F32),
            V((64, 128), F32), V((7, 8, 128), F32),
            V((NZ, 8, 128), F32), V((NY, 8, 128), F32), V((32, 128), F32),
            dma((9,)), *[dma((n,)) for n in (4, 4, 8, 8, 3, 3, 7, 7, 7, 7, 3, 3, 8, 8, 4, 4)],
            *[dma((n,)) for n in (7, 7, 7, 7, 7, 7, 3, 3)],
            *[dma((n,)) for n in (7, 7, 8, 8, 24, 24, 4, 4, 4, 4, 3, 3, 7, 7, 8, 8)], dma((4,)),
            *[dma] * 4,
        ],
        compiler_params=pltpu.CompilerParams(
            collective_id=0, has_side_effects=True, vmem_limit_bytes=32 * 1024 * 1024),
        name="exchange",
    )(*[pltpu.with_memory_space_constraint(a, pltpu.HBM) for a in (ug, ue, up_warm.T, dg, de, down_warm.T)])
    ua, ur, da, dr = pl.pallas_call(
        finish,
        out_shape=(
            jax.ShapeDtypeStruct((UP_R, UP_C), BF16),
            jax.ShapeDtypeStruct((UP_R, UP_C), F32),
            jax.ShapeDtypeStruct((DN_R, DN_C), BF16),
            jax.ShapeDtypeStruct((DN_R, DN_C), F32),
        ),
        in_specs=[vm] * 7,
        out_specs=(anywhere,) * 4,
        scratch_shapes=[
            V((UP_R, UP_C), BF16), V((UP_R, UP_C), F32), V((DN_R, DN_C), BF16), V((DN_R, DN_C), F32), dma((20,)),
        ],
        compiler_params=pltpu.CompilerParams(vmem_limit_bytes=32 * 1024 * 1024),
        name="finish",
    )(fa0, fa1, fb, wu, wd, mu, md)
    return ua, ur[None], da, dr[None]


def solution(mesh):
    return jax.shard_map(
        body,
        mesh=mesh,
        in_specs=(
            P("dp", None, "mp"),
            P("dp", None, "mp"),
            P("mp", None),
            P("dp", None, "mp"),
            P("dp", None, "mp"),
            P("mp", None),
        ),
        out_specs=(P(None, "mp"), P("dp", None, "mp"), P(None, "mp"), P("dp", None, "mp")),
        check_vma=False,
    )
```

```python
import jax
import jax.numpy as jnp
from jax import lax
from jax.experimental import pallas as pl
from jax.experimental.pallas import tpu as pltpu
from jax.sharding import PartitionSpec as P

F32 = jnp.float32
BF16 = jnp.bfloat16
HI = lax.Precision.HIGHEST
MESH = pl.DeviceIdType.MESH
NY, NX, NC, NZ = 8, 4, 2, 8
RANK = 32
UP_R, UP_C = 64, 3584
DN_R, DN_C = 128, 1024
HALF = UP_C // 2


def nt(a, b, precision=None):
    return lax.dot_general(a, b, (((1,), (1,)), ((), ())), preferred_element_type=F32, precision=precision)


def split(a):
    hi = a.astype(BF16)
    return hi, (a - hi.astype(F32)).astype(BF16)


def nt3(a, b):
    ah, al = split(a)
    bh, bl = split(b)
    return nt(ah, bh) + nt(ah, bl) + nt(al, bh)


def nt_acc(acc, wide, a, b):
    bh, bl = split(b)
    both = nt(wide, bh)
    return acc + both[:RANK] + both[RANK:] + nt(a, bl)


def eliminate(arrays, where, off):
    shape = (RANK, 128)
    row = lax.broadcasted_iota(jnp.int32, shape, 0)
    scale = jnp.ones(shape, F32)
    for first in range(0, RANK, 8):
        cols = [jnp.broadcast_to(arrays[where][:, off + first + m:off + first + m + 1], shape) for m in range(8)]
        for m in range(8):
            k = first + m
            pivot = cols[m][k:k + 1, :]
            factor = jnp.where(row > k, cols[m] * (1.0 / pivot), 0.0)
            for n in range(m + 1, 8):
                cols[n] = cols[n] - factor * cols[n][k:k + 1, :]
            arrays = [a - factor * a[k:k + 1, :] for a in arrays]
            scale = jnp.where(row == k, lax.rsqrt(pivot), scale)
    return arrays[0] * scale


def exchange(ug, ue, uw, dg, de, dw, FA0, FA1, FB, wu_out, wd_out, mu_out, md_out,
             MU, MD,
             vug, vue, vuw, vdg, vde, vdw, TU0, TU1, TD0, TD1, CU0, CU1, CD, XU0, XU1, YD, YU0, YU1, XD0, XD1,
             SA0, SA1, SB, SW, pt, pxr, pz, py, pg,
             in_sem, s_cu, r_cu, s_cd, r_cd, s_xu, r_xu, s_yd, r_yd, s_yu, r_yu, s_xd, r_xd, s_vu, r_vu, s_vd, r_vd,
             s_px, r_px, s_pz, r_pz, s_py, r_py, s_pa, r_pa,
             s_ay, r_ay, s_a1, r_a1, s_ax, r_ax, s_ac, r_ac, s_ad, r_ad, s_bx, r_bx, s_by, r_by, s_bc, r_bc, own_sem,
             s_wu, r_wu, s_wd, r_wd):
    d = lax.axis_index("dp")
    z = lax.axis_index("mp")
    c = lax.rem(d, 2)
    x = lax.rem(lax.div(d, 2), NX)
    y = lax.div(d, 8)
    other = 1 - c
    far_y = (4, 3, 5, 2, 6, 1, 7)
    far_x = (2, 1, 3)

    def at(yy, xx, cc):
        return ((yy * NX + xx) * NC + cc, z)

    partner = at(y, x, other)

    xs = [lax.rem(x + o, NX) for o in range(NX)]
    ys = [lax.rem(y + o, NY) for o in range(NY)]
    zs = [lax.rem(z + o, NZ) for o in range(NZ)]

    def xof(o):
        return xs[o % NX]

    def yof(o):
        return ys[o % NY]

    def xpeer(o):
        return at(y, xof(o), c)

    def ypeer(o):
        return at(yof(o), x, c)

    def zpeer(o):
        return (d, zs[o])

    pairs = []
    for half in range(2):
        cols = pl.ds(half * HALF, HALF)
        pairs += [(ug.at[:, cols], vug.at[:, cols]), (ue.at[:, cols], vue.at[:, cols]), (uw.at[:, cols], vuw.at[:, cols])]
    pairs += [(dg, vdg), (de, vde), (dw, vdw)]
    loads = [pltpu.make_async_copy(a, b, in_sem.at[i]) for i, (a, b) in enumerate(pairs)]
    bar = pltpu.get_barrier_semaphore()

    def greet(dev):
        pl.semaphore_signal(bar, 1, device_id=dev, device_id_type=MESH)

    for o in far_y[:3]:
        greet(zpeer(o))
        greet(ypeer(o))
    for cp in loads:
        cp.start()
    for o in far_y[3:]:
        greet(zpeer(o))
        greet(ypeer(o))
    for o in far_x:
        greet(at(y, xs[o], other))
        greet(xpeer(o))
    greet(partner)

    def down_part(b):
        cols = pl.ds(256 * b, 256)
        return vdg[:, cols].astype(F32) + vde[:, cols]

    def up_part(half, b):
        cols = pl.ds(half * HALF + 256 * b, 256)
        return vug[:, cols].astype(F32) + vue[:, cols]

    acc = jnp.zeros((RANK, UP_R), F32)
    for half in range(2):
        for cp in loads[3 * half:3 * half + 3]:
            cp.wait()
        for b in range(HALF // 256):
            hi, lo = split(vuw[:, pl.ds(half * HALF + 256 * b, 256)])
            acc = nt_acc(acc, jnp.concatenate([hi, lo], axis=0), hi, up_part(half, b))
    pt[0:32, :] = jnp.concatenate([acc, jnp.zeros((RANK, 64), F32)], axis=1)
    for cp in loads[6:]:
        cp.wait()
    acc = jnp.zeros((RANK, DN_R), F32)
    for b in range(DN_C // 256):
        hi, lo = split(vdw[:, pl.ds(256 * b, 256)])
        acc = nt_acc(acc, jnp.concatenate([hi, lo], axis=0), hi, down_part(b))
    pt[32:64, :] = acc

    pl.semaphore_wait(bar, 7 + 7 + 7)

    def describe(src, dst, ssem, rsem, dev):
        return pltpu.make_async_remote_copy(src_ref=src, dst_ref=dst, send_sem=ssem, recv_sem=rsem,
                                            device_id=dev, device_id_type=MESH)

    def remote(log, src, dst, ssem, rsem, dev):
        cp = describe(src, dst, ssem, rsem, dev)
        cp.start()
        log.append(cp)
        return cp

    sent = []
    cp_px = []
    for o, cc, k in ((2, other, 5), (2, c, 1), (1, other, 4), (3, other, 6), (1, c, 0), (3, c, 2), (0, other, 3)):
        rows = pl.ds(pl.multiple_of(cc * 32 + xs[o] * 8, 8), 8)
        cp_px.append(remote(sent, pt.at[rows], pxr.at[k], s_px.at[k], r_px.at[k], at(y, xs[o], cc)))

    for b in range(HALF // 256):
        parts = [up_part(0, b), up_part(1, b)]
        for half in range(2):
            MU[:, half * HALF + 256 * b:half * HALF + 256 * b + 256] = parts[half]
        stacked = jnp.concatenate(parts, axis=0)
        for s in range(2):
            turned = stacked[:, 128 * s:128 * (s + 1)].T
            for i in range(16):
                tile = (2 * b + s) * 16 + i
                q, u = tile // 7, tile % 7
                dst, r0 = (TU0, 8 * u) if u < 4 else (TU1, 8 * u - 32)
                dst[q // NY, q % NY, r0:r0 + 8, :] = turned[8 * i:8 * i + 8, :]

    for b in range(DN_C // 256):
        m = down_part(b)
        MD[:, 256 * b:256 * b + 256] = m
        for s in range(2):
            turned = m[:, 128 * s:128 * (s + 1)].T
            for i in range(4):
                q = (2 * b + s) * 4 + i
                TD0[q // NX, q % NX] = turned[32 * i:32 * i + 16, :]
                TD1[q // NX, q % NX] = turned[32 * i + 16:32 * i + 32, :]

    keep = [pltpu.make_async_copy(MU, mu_out, own_sem.at[2]), pltpu.make_async_copy(MD, md_out, own_sem.at[3])]
    for cp in keep:
        cp.start()
    mine = pl.ds(pl.multiple_of(x * 8, 8), 8)

    def proj_z(log):
        for cp in cp_px:
            cp.wait_recv()
        own = pt[pl.ds(pl.multiple_of(c * 32 + x * 8, 8), 8), :]
        pz[z] = ((own + pxr[0]) + (pxr[1] + pxr[2])) + ((pxr[3] + pxr[4]) + (pxr[5] + pxr[6]))
        return [remote(log, pz.at[z], pz.at[z], s_pz.at[o - 1], r_pz.at[o - 1], zpeer(o)) for o in far_y]

    def proj_y(log, cps):
        for cp in cps:
            cp.wait_recv()
        py[y] = ((pz[0] + pz[1]) + (pz[2] + pz[3])) + ((pz[4] + pz[5]) + (pz[6] + pz[7]))
        return [remote(log, py.at[y], py.at[y], s_py.at[o - 1], r_py.at[o - 1], ypeer(o)) for o in far_y]

    def proj_x(log, cps):
        for cp in cps:
            cp.wait_recv()
        pg[mine, :] = ((py[0] + py[1]) + (py[2] + py[3])) + ((py[4] + py[5]) + (py[6] + py[7]))
        return [remote(log, pg.at[mine], pg.at[mine], s_pa.at[o - 1], r_pa.at[o - 1], xpeer(o)) for o in far_x]

    lane = lax.broadcasted_iota(jnp.int32, (RANK, 128), 1)
    lane16 = lane[0:16]
    lane8 = lane[0:8]

    def local(log, src, dst, sem):
        cp = pltpu.make_async_copy(src, dst, sem)
        cp.start()
        log.append(cp)
        return cp

    def sum_merged(core, log):
        tu, tu_other = (TU0, TU1) if core == 0 else (TU1, TU0)
        td, td_other = (TD0, TD1) if core == 0 else (TD1, TD0)
        cu, cu_other = (CU0, CU1) if core == 0 else (CU1, CU0)
        xu = XU0 if core == 0 else XU1
        order = [(0, 2), (1, 4), (1, 3), (1, 5), (0, 1), (1, 2), (1, 6), (0, 3), (1, 1), (1, 7), (0, 0), (1, 0)]
        for kind, o in order:
            if kind == 0:
                remote(log, tu_other.at[xs[o]], cu_other.at[xs[o]], s_cu.at[o], r_cu.at[o], partner)
            else:
                remote(log, td_other.at[ys[o]], CD.at[ys[o]], s_cd.at[o], r_cd.at[o], partner)
        cp_xu, cp_yd = [], []
        for kind, o in order:
            if kind == 0:
                xx = xs[o]
                describe(tu.at[xx], cu.at[xx], s_cu.at[o], r_cu.at[o], partner).wait_recv()
                tu[xx] = tu[xx] + cu[xx]
                if o:
                    cp_xu.append(remote(log, tu.at[xx], xu.at[o - 1], s_xu.at[o - 1], r_xu.at[o - 1], xpeer(o)))
            else:
                yy = ys[o]
                describe(td.at[yy], CD.at[yy], s_cd.at[o], r_cd.at[o], partner).wait_recv()
                td[yy] = td[yy] + CD[yy]
                if o:
                    cp_yd.append(remote(log, td.at[yy], YD.at[o - 1], s_yd.at[o - 1], r_yd.at[o - 1], ypeer(o)))

        cp_py = proj_y(log, proj_z(log))

        for cp in cp_xu:
            cp.wait_recv()
        for o in far_y + (0,):
            yy = ys[o]
            tu[x, yy] = (tu[x, yy] + xu[0, yy]) + (xu[1, yy] + xu[2, yy])
            if core == 1:
                remote(log, tu.at[x, yy], YU1.at[o], s_vu.at[o], r_vu.at[o], at(yy, x, 0))
            elif o:
                remote(log, tu.at[x, yy], YU0.at[o - 1], s_yu.at[o - 1], r_yu.at[o - 1], at(yy, x, 0))

        cp_pa = proj_x(log, cp_py)

        for cp in cp_yd:
            cp.wait_recv()
        for o in far_x + (0,):
            xx = xs[o]
            tot = td[y, xx]
            for i in range(NY - 1):
                tot = tot + YD[i, xx]
            td[y, xx] = tot
            if core == 0:
                remote(log, td.at[y, xx], XD0.at[o], s_vd.at[o], r_vd.at[o], at(y, xx, 1))
            elif o:
                remote(log, td.at[y, xx], XD1.at[o - 1], s_xd.at[o - 1], r_xd.at[o - 1], at(y, xx, 1))
        for cp in cp_pa:
            cp.wait_recv()

    def pass_on(log, ref, k):
        return [remote(log, ref.at[x, ys[k]], ref.at[x, ys[k]], s_ax.at[8 * (o - 1) + k], r_ax.at[8 * (o - 1) + k],
                       xpeer(o)) for o in far_x]

    def gathered(cps):
        for cp in cps:
            cp.wait_recv()

    near_y = (1, 7, 2, 6, 3, 5, 4)

    @pl.when(c == 0)
    def _():
        log, near = [], []
        sum_merged(0, log)
        a = pg[...]
        gram = nt(a, a, HI)
        a = eliminate([jnp.concatenate([a[:, :64], gram, jnp.zeros((RANK, 32), F32)], axis=1)], 0, 64)
        left = jnp.where(lane < 64, a, 0.0)
        right = pltpu.roll(left, 64, axis=1)
        w = jnp.concatenate([left, right, left, right], axis=0)
        for o in far_y:
            describe(TU0.at[x, y], YU0.at[o - 1], s_yu.at[o - 1], r_yu.at[o - 1], partner).wait_recv()
        for o in far_y + (0,):
            describe(TU1.at[x, y], YU1.at[o], s_vu.at[o], r_vu.at[o], partner).wait_recv()
        low = TU0[x, y]
        for i in range(NY - 1):
            low = low + YU0[i]
        high = YU1[0]
        for i in range(1, NY):
            high = high + YU1[i]
        r = nt(jnp.concatenate([low, high], axis=0) * (1.0 / 64.0), w, HI)
        SA1[...] = jnp.where(lane16 < 64, r[16:32], jnp.concatenate([r[48:56], jnp.zeros((8, 128), F32)], axis=0))
        SA0[...] = jnp.where(lane16 < 64, r[0:16], r[32:48])

        before = len(log)
        cp_ay = {}
        remote(log, SA1, FA1.at[x, y], s_a1.at[0], r_a1.at[0], partner)
        for o in far_y:
            remote(log, SA1, FA1.at[x, y], s_a1.at[o], r_a1.at[o], at(ys[o], x, 1))
            cp_ay[o] = remote(log, SA0, FA0.at[x, y], s_ay.at[o - 1], r_ay.at[o - 1], ypeer(o))
        local(near, SA0, FA0.at[x, y], own_sem.at[0])
        near[0].wait()
        pieces = [pass_on(log, FA0, 0)]
        for k in near_y:
            cp_ay[NY - k].wait_recv()
            pieces.append(pass_on(log, FA0, k))
        remote(log, FA0.at[x], FA0.at[x], s_ac.at[0], r_ac.at[0], partner)
        SW[...] = w.T
        remote(log, SW, wu_out, s_wu, r_wu, partner)
        local(near, SW, wu_out, own_sem.at[1])
        for cp in sent + log[:before]:
            cp.wait_send()
        for cp in keep:
            cp.wait()
        for i, o in ((1, 1), (2, 3), (0, 2)):
            gathered([p[i] for p in pieces])
            xx = xof(NX - o)
            remote(log, FA0.at[xx], FA0.at[xx], s_ac.at[o], r_ac.at[o], partner)
        describe(SW, wd_out, s_wd, r_wd, partner).wait_recv()
        for o in range(NY):
            describe(FB.at[ys[o]], FB.at[ys[o]], s_bc.at[o], r_bc.at[o], partner).wait_recv()
        for o in range(NX):
            describe(FA1.at[xs[o]], FA1.at[xs[o]], s_ad.at[o], r_ad.at[o], partner).wait_recv()
        for cp in log[before:]:
            cp.wait_send()
        near[1].wait()

    @pl.when(c == 1)
    def _():
        log, near = [], []
        sum_merged(1, log)
        a = pg[...]
        gram = nt(a, a, HI)
        a = eliminate([a, jnp.concatenate([gram, jnp.zeros((RANK, 96), F32)], axis=1)], 1, 0)
        w = jnp.concatenate([a, a, a, a], axis=0)
        for o in far_x:
            describe(TD1.at[y, x], XD1.at[o - 1], s_xd.at[o - 1], r_xd.at[o - 1], partner).wait_recv()
        for o in far_x + (0,):
            describe(TD0.at[y, x], XD0.at[o], s_vd.at[o], r_vd.at[o], partner).wait_recv()
        low = (XD0[0] + XD0[1]) + (XD0[2] + XD0[3])
        high = (TD1[y, x] + XD1[0]) + (XD1[1] + XD1[2])
        r = nt(jnp.concatenate([low, high], axis=0) * (1.0 / 64.0), w, HI)
        low = jnp.where(lane8 < 32, r[0:8], r[8:16])
        high = jnp.where(lane8 < 96, r[16:24], r[24:32])
        SB[...] = jnp.where(lane8 < 64, low, high)

        before = len(log)
        cp_bx = [remote(log, SB, FB.at[y, x], s_bx.at[o - 1], r_bx.at[o - 1], xpeer(o)) for o in far_x]
        local(near, SB, FB.at[y, x], own_sem.at[0])
        SW[...] = w.T
        remote(log, SW, wd_out, s_wd, r_wd, partner)
        local(near, SW, wd_out, own_sem.at[1])
        near[0].wait()
        pieces = []
        for k in (0,) + near_y:
            o = (NY - k) % NY
            describe(SA1, FA1.at[x, ys[k]], s_a1.at[o], r_a1.at[o], partner).wait_recv()
            pieces.append(pass_on(log, FA1, k))
            if k == 7:
                for cp in cp_bx:
                    cp.wait_recv()
                cp_by = [remote(log, FB.at[y], FB.at[y], s_by.at[p - 1], r_by.at[p - 1], ypeer(p)) for p in far_y]
        remote(log, FA1.at[x], FA1.at[x], s_ad.at[0], r_ad.at[0], partner)
        remote(log, FB.at[y], FB.at[y], s_bc.at[0], r_bc.at[0], partner)
        for cp in sent + log[:before]:
            cp.wait_send()
        for cp in keep:
            cp.wait()
        for cp, o in zip(cp_by, far_y):
            cp.wait_recv()
            yy = yof(NY - o)
            remote(log, FB.at[yy], FB.at[yy], s_bc.at[o], r_bc.at[o], partner)
        for i, o in ((1, 1), (2, 3), (0, 2)):
            gathered([p[i] for p in pieces])
            xx = xof(NX - o)
            remote(log, FA1.at[xx], FA1.at[xx], s_ad.at[o], r_ad.at[o], partner)
        describe(SW, wu_out, s_wu, r_wu, partner).wait_recv()
        for o in range(NX):
            describe(FA0.at[xs[o]], FA0.at[xs[o]], s_ac.at[o], r_ac.at[o], partner).wait_recv()
        for cp in log[before:]:
            cp.wait_send()
        near[1].wait()


def finish(fa0, fa1, fb, wu, wd, mu, md, ua, ur, da, dr, bua, bur, bda, bdr, sem):
    lane = lax.broadcasted_iota(jnp.int32, (8, 128), 1)
    started = []

    def store(src, dst, cols):
        cp = pltpu.make_async_copy(src.at[:, cols], dst.at[:, cols], sem.at[len(started)])
        cp.start()
        started.append(cp)

    def up_tile(tile):
        q, u = tile // 7, tile % 7
        src, r0 = (fa0, fa1)[u % 4 // 2], (u % 2) * 8
        return jnp.where(lane // 64 == u // 4, src[q // NY, q % NY, r0:r0 + 8, :], 0.0)

    def down_tile(tile):
        q, u = tile // 4, tile % 4
        return jnp.where(lane // 32 == u, fb[q // NX, q % NX], 0.0)

    for first, last in ((0, 2), (2, 4), (4, 6), (6, 7)):
        for b in range(first, last):
            delta = nt3(wu[...], jnp.concatenate([up_tile(32 * b + i) for i in range(32)], axis=0))
            for half in range(2):
                cols = pl.ds(half * HALF + 256 * b, 256)
                part = delta[64 * half:64 * half + 64, :]
                bua[:, cols] = part.astype(BF16)
                bur[:, cols] = mu[:, cols] - part
        for half in range(2):
            cols = pl.ds(half * HALF + 256 * first, 256 * (last - first))
            store(bua, ua, cols)
            store(bur, ur, cols)
    for first, last in ((0, 2), (2, 4)):
        for b in range(first, last):
            cols = pl.ds(256 * b, 256)
            delta = nt3(wd[...], jnp.concatenate([down_tile(32 * b + i) for i in range(32)], axis=0))
            bda[:, cols] = delta.astype(BF16)
            bdr[:, cols] = md[:, cols] - delta
        cols = pl.ds(256 * first, 256 * (last - first))
        store(bda, da, cols)
        store(bdr, dr, cols)
    for cp in started:
        cp.wait()


def body(up_grad, up_error, up_warm, down_grad, down_error, down_warm):
    ug, ue, dg, de = up_grad[0], up_error[0], down_grad[0], down_error[0]
    vm = pl.BlockSpec(memory_space=pltpu.VMEM)
    hbm = pl.BlockSpec(memory_space=pltpu.HBM)
    anywhere = pl.BlockSpec(memory_space=pl.ANY)
    dma = pltpu.SemaphoreType.DMA
    V = pltpu.VMEM
    fa0, fa1, fb, wu, wd, mu, md = pl.pallas_call(
        exchange,
        out_shape=(
            jax.ShapeDtypeStruct((NX, NY, 16, 128), F32),
            jax.ShapeDtypeStruct((NX, NY, 16, 128), F32),
            jax.ShapeDtypeStruct((NY, NX, 8, 128), F32),
            jax.ShapeDtypeStruct((128, 128), F32),
            jax.ShapeDtypeStruct((128, 128), F32),
            jax.ShapeDtypeStruct((UP_R, UP_C), F32),
            jax.ShapeDtypeStruct((DN_R, DN_C), F32),
        ),
        in_specs=[hbm] * 6,
        out_specs=(anywhere,) * 7,
        scratch_shapes=[
            V((UP_R, UP_C), F32), V((DN_R, DN_C), F32),
            V((UP_R, UP_C), BF16), V((UP_R, UP_C), F32), V((RANK, UP_C), F32),
            V((DN_R, DN_C), BF16), V((DN_R, DN_C), F32), V((RANK, DN_C), F32),
            V((NX, NY, 32, 128), F32), V((NX, NY, 24, 128), F32), V((NY, NX, 16, 128), F32), V((NY, NX, 16, 128), F32),
            V((NX, NY, 32, 128), F32), V((NX, NY, 24, 128), F32), V((NY, NX, 16, 128), F32),
            V((NX - 1, NY, 32, 128), F32), V((NX - 1, NY, 24, 128), F32), V((NY - 1, NX, 16, 128), F32),
            V((NY - 1, 32, 128), F32), V((NY, 24, 128), F32), V((NX, 16, 128), F32), V((NX - 1, 16, 128), F32),
            V((16, 128), F32), V((16, 128), F32), V((8, 128), F32), V((128, 128), F32),
            V((64, 128), F32), V((7, 8, 128), F32),
            V((NZ, 8, 128), F32), V((NY, 8, 128), F32), V((32, 128), F32),
            dma((9,)), *[dma((n,)) for n in (4, 4, 8, 8, 3, 3, 7, 7, 7, 7, 3, 3, 8, 8, 4, 4)],
            *[dma((n,)) for n in (7, 7, 7, 7, 7, 7, 3, 3)],
            *[dma((n,)) for n in (7, 7, 8, 8, 24, 24, 4, 4, 4, 4, 3, 3, 7, 7, 8, 8)], dma((4,)),
            *[dma] * 4,
        ],
        compiler_params=pltpu.CompilerParams(
            collective_id=0, has_side_effects=True, vmem_limit_bytes=32 * 1024 * 1024),
        name="exchange",
    )(*[pltpu.with_memory_space_constraint(a, pltpu.HBM) for a in (ug, ue, up_warm.T, dg, de, down_warm.T)])
    ua, ur, da, dr = pl.pallas_call(
        finish,
        out_shape=(
            jax.ShapeDtypeStruct((UP_R, UP_C), BF16),
            jax.ShapeDtypeStruct((UP_R, UP_C), F32),
            jax.ShapeDtypeStruct((DN_R, DN_C), BF16),
            jax.ShapeDtypeStruct((DN_R, DN_C), F32),
        ),
        in_specs=[vm] * 7,
        out_specs=(anywhere,) * 4,
        scratch_shapes=[
            V((UP_R, UP_C), BF16), V((UP_R, UP_C), F32), V((DN_R, DN_C), BF16), V((DN_R, DN_C), F32), dma((20,)),
        ],
        compiler_params=pltpu.CompilerParams(vmem_limit_bytes=32 * 1024 * 1024),
        name="finish",
    )(fa0, fa1, fb, wu, wd, mu, md)
    return ua, ur[None], da, dr[None]


def solution(mesh):
    return jax.shard_map(
        body,
        mesh=mesh,
        in_specs=(
            P("dp", None, "mp"),
            P("dp", None, "mp"),
            P("mp", None),
            P("dp", None, "mp"),
            P("dp", None, "mp"),
            P("mp", None),
        ),
        out_specs=(P(None, "mp"), P("dp", None, "mp"), P(None, "mp"), P("dp", None, "mp")),
        check_vma=False,
    )
```
